32 devices in a mesh: row: 8 (over z, y), col: 4 (over x, core).
Axes of the slice: x: 2, y: 2, z: 4, core: 2. Of those that a mesh axis runs over, the one named last changes fastest.
Arguments:
- covariance: bfloat16 [28672, 28672], P('row', 'col'), may hold values from -1 to 8, as said below
- right_side: float32 [28672, 256], P(('col', 'row')), may hold values from -50 to 50
Outputs:
- solution: float32 [28672, 256], P(('col', 'row'))
- residual: float32 [28672, 256], P(('col', 'row'))
- direction: float32 [28672, 256], P(('col', 'row'))
The draws below stay inside these ranges and needn't reach their ends.
Inputs may be any that keep to these rules, and one draw needn't show every extreme that they name: `covariance`: symmetric and positive definite, with condition number under 100.
All inputs are finite; a program needn't handle non-finite values.
Results may differ from the reference program's by a relative error of at most 0.0158.
Values may be sent and summed in bfloat16 or wider, within the bound.
No kernel may reach another device: no remote copies, remote signals or barrier semaphores. Data moves between devices by JAX's collectives and lax.ppermute only.
A program may use at most 128 MiB of HBM per device.

```python
import math
import jax
import jax.numpy as jnp
from jax import lax

ORDER = 28672
EDITS = 256
ITERS = 3


def draw_covariance(key, part):
    first_key, second_key = jax.random.split(jax.random.fold_in(key, 11))
    radius = 0.7
    top_scale = 4.0
    factor = radius / (2.0 * math.sqrt(2.0 * ORDER / 3.0))
    entries = jax.random.uniform(first_key, (ORDER, ORDER), jnp.float32, -1.0, 1.0)
    symmetric = (entries + entries.T) * factor
    positions = jnp.arange(ORDER)
    symmetric = symmetric.at[positions, positions].set(1.0)
    scales = jnp.sqrt(jnp.exp(jax.random.uniform(second_key, (ORDER,), jnp.float32, 0.0, math.log(top_scale))))
    return (symmetric * scales[:, None] * scales[None, :]).astype(jnp.bfloat16)


def draw_right_side(key, part):
    first_key, second_key = jax.random.split(jax.random.fold_in(key, 23), 2)
    row_pos = jnp.arange(ORDER).astype(jnp.float32) / ORDER
    row_scale = jnp.exp(math.log(10.0) * row_pos)
    col_scale = jnp.exp(jax.random.uniform(second_key, (EDITS,), jnp.float32, 0.0, math.log(10.0)))
    base_part = jax.random.normal(first_key, (ORDER, EDITS), jnp.float32)
    base_part = jnp.clip(base_part, -5.0, 5.0)
    return base_part * row_scale[:, None] * col_scale[None, :] * 0.1


def setup_inputs(seed: int = 0) -> dict:
    seeds = jax.random.split(jax.random.key(seed), 3)
    return {
        "covariance": draw_covariance(jax.random.fold_in(seeds[2], 71), 0),
        "right_side": draw_right_side(jax.random.fold_in(seeds[2], 71), 0),
    }


HIGHEST_PRECISION = lax.Precision.HIGHEST

def inner_product(left_block, right_block):
    return lax.dot_general(left_block.astype(jnp.float32), right_block.astype(jnp.float32), (((0,), (0,)), ((), ())), precision=HIGHEST_PRECISION, preferred_element_type=jnp.float32)

def apply_small(block, coeffs):
    return jnp.dot(block.astype(jnp.float32), coeffs.astype(jnp.float32), precision=HIGHEST_PRECISION, preferred_element_type=jnp.float32)

def symmetric_part(matrix):
    return 0.5 * (matrix + matrix.T)

def solve_spd(matrix, rhs_block):
    factor = jnp.linalg.cholesky(matrix)
    return jax.scipy.linalg.cho_solve((factor, True), rhs_block)

def covariance_times(covariance, lowered):
    strip_rows = math.gcd(ORDER, 1024)
    strips = covariance.reshape(ORDER // strip_rows, strip_rows, ORDER)
    widened = lowered.astype(jnp.float32)

    def one_strip(strip):
        return jnp.dot(strip.astype(jnp.float32), widened.astype(jnp.float32), precision=HIGHEST_PRECISION, preferred_element_type=jnp.float32)
    stacked = lax.map(one_strip, strips)
    return stacked.reshape(ORDER, EDITS)

def reference(covariance, right_side):
    solution = jnp.zeros_like(right_side)
    residual = right_side
    direction = right_side
    norm_now = inner_product(residual, residual)
    for iteration in range(ITERS):
        lowered = direction.astype(jnp.bfloat16)
        image = covariance_times(covariance, lowered)
        curvature = symmetric_part(inner_product(direction, image))
        alpha = solve_spd(curvature, norm_now)
        solution = solution + apply_small(direction, alpha)
        residual = residual - apply_small(image, alpha)
        norm_next = inner_product(residual, residual)
        beta = solve_spd(norm_now, norm_next)
        direction = residual + apply_small(direction, beta)
        norm_now = norm_next
    return (solution, residual, direction)
```

```python
import functools

import jax
import jax.numpy as jnp
import numpy as np
from jax import lax
from jax.experimental import pallas as pl
from jax.experimental.pallas import tpu as pltpu
from jax.sharding import PartitionSpec as P

ITERS = 3
AXES = ("row", "col")
HIGHEST = lax.Precision.HIGHEST
VMEM_LIMIT = 48 * 1024 * 1024
DONE = 1e-13
MAX_SQUARINGS = 48


def dot(left, right):
    return jnp.dot(left, right, precision=HIGHEST, preferred_element_type=jnp.float32)


def send(block, pairs):
    return lax.ppermute(block, AXES, pairs)


def vmem_params(**extra):
    return pltpu.CompilerParams(vmem_limit_bytes=VMEM_LIMIT, **extra)


def bits_of(size, first_stride):
    assert size & (size - 1) == 0
    return [first_stride << b for b in range(size.bit_length() - 1)]


def ring_order(rows):
    fast = 1 << ((rows.bit_length() - 1) // 2)
    slow = rows // fast
    if fast == 1 or slow == 1:
        return list(range(rows))
    cycle = [s * fast for s in range(slow)]
    for s in reversed(range(slow)):
        lane = range(1, fast) if (slow - 1 - s) % 2 == 0 else reversed(range(1, fast))
        cycle += [s * fast + f for f in lane]
    return cycle


def chunk_kernel(blocks, has_base, index_ref, *refs):
    covs, parts = refs[:blocks], refs[blocks : 2 * blocks]
    out = refs[-1]
    total = refs[2 * blocks][...] if has_base else None
    for cov, part in zip(covs, parts):
        term = jnp.dot(cov[...], part[...], preferred_element_type=jnp.float32)
        total = term if total is None else total + term
    out[...] = total


def add_chunks(covariance, row_blocks, owners, parts, base, height):
    blocks = len(parts)
    depth, edits = parts[0].shape
    count = row_blocks.shape[0]
    index = jnp.concatenate([jnp.stack(owners).astype(jnp.int32), row_blocks])
    cov_specs = [
        pl.BlockSpec((height, depth), functools.partial(lambda t, i, ix: (ix[blocks + i], ix[t]), t))
        for t in range(blocks)
    ]
    part_specs = [pl.BlockSpec((depth, edits), lambda i, ix: (0, 0)) for _ in parts]
    row_spec = pl.BlockSpec((height, edits), lambda i, ix: (i, 0))
    has_base = base is not None
    operands = [covariance] * blocks + list(parts) + ([base] if has_base else [])
    return pl.pallas_call(
        functools.partial(chunk_kernel, blocks, has_base),
        grid_spec=pltpu.PrefetchScalarGridSpec(
            num_scalar_prefetch=1,
            grid=(count,),
            in_specs=cov_specs + part_specs + ([row_spec] if has_base else []),
            out_specs=row_spec,
        ),
        out_shape=jax.ShapeDtypeStruct((count * height, edits), jnp.float32),
        input_output_aliases={1 + 2 * blocks: 0} if has_base else {},
        compiler_params=vmem_params(),
        cost_estimate=pl.CostEstimate(
            flops=2 * count * height * depth * blocks * edits,
            bytes_accessed=2 * count * height * depth * blocks,
            transcendentals=0,
        ),
    )(index, *operands)


def partial_image(covariance, lowered, order, cols):
    rows = len(order)
    depth = lowered.shape[0]
    quarter = covariance.shape[0] // cols
    me_row, me_col = lax.axis_index("row"), lax.axis_index("col")
    if depth % 128 or depth % 32 or quarter % 16 or rows % 2:
        whole = lax.all_gather(lowered, "row", axis=0, tiled=True)
        product = jnp.dot(covariance, whole, preferred_element_type=jnp.float32)
        swapped = product.reshape(cols, quarter, -1)[jnp.arange(cols) ^ me_col]
        return swapped.reshape(product.shape)
    split = 2 if quarter % 32 == 0 and quarter > 512 else 1
    height = quarter // split
    lane = jnp.arange(cols * split, dtype=jnp.int32)
    row_blocks = ((lane // split) ^ me_col) * split + lane % split
    place = [order.index(r) for r in range(rows)]
    forward = [
        (r * cols + c, order[(place[r] + 1) % rows] * cols + c) for r in range(rows) for c in range(cols)
    ]
    backward = [(b, a) for a, b in forward]
    cycle, where = jnp.array(order, jnp.int32), jnp.array(place, jnp.int32)[me_row]

    def owner(shift):
        return cycle[(where + shift) % rows]

    ahead = behind = lowered
    held, owners, total = [lowered], [me_row], None
    for step in range(1, rows // 2 + 1):
        if step < rows // 2:
            behind, ahead = send(behind, forward), send(ahead, backward)
            arrived, names = [behind, ahead], [owner(-step), owner(step)]
        else:
            half = depth // 2
            low, high = send(behind[:half], forward), send(ahead[half:], backward)
            arrived, names = [jnp.concatenate([low, high])], [owner(step)]
        total = add_chunks(covariance, row_blocks, owners, held, total, height)
        held, owners = arrived, names
    return add_chunks(covariance, row_blocks, owners, held, total, height)


def exchange_sum(total, cols):
    quarter = total.shape[0] // cols
    pieces = {j: total[j * quarter : (j + 1) * quarter] for j in range(cols)}
    rows = lax.axis_size("row")
    strides = bits_of(cols, 1)
    for bit in strides:
        pairs = [(i, i ^ bit) for i in range(rows * cols)]
        last = bit == strides[-1]
        got = {}
        for j in sorted((j for j in pieces if j & bit), reverse=True):
            block = pieces[j].astype(jnp.bfloat16) if bit > 1 else pieces[j]
            got[j ^ bit] = send(block, pairs)
        if last:
            return pieces[0], got[0]
        pieces = {j: pieces[j] + got[j].astype(jnp.float32) for j in got}
    return pieces[0], jnp.zeros_like(pieces[0])


def gram_kernel(first, own, got, residual, *refs):
    direction = None if first else refs[0]
    image, grams = refs[-2:]
    value = own[...] + got[...].astype(jnp.float32)
    image[...] = value
    order = value.shape[1]
    flipped = value.T
    grams[0:order] = dot(flipped, value)
    grams[order : 2 * order] = dot(flipped, residual[...])
    if first:
        grams[2 * order :] = dot(residual[...].T, residual[...])
    else:
        grams[2 * order :] = dot(flipped, direction[...])


def local_grams(own, got, residual, direction, first):
    rows, edits = own.shape
    operands = [own, got, residual] + ([] if first else [direction])
    return pl.pallas_call(
        functools.partial(gram_kernel, first),
        out_shape=[
            jax.ShapeDtypeStruct((rows, edits), jnp.float32),
            jax.ShapeDtypeStruct((3 * edits, edits), jnp.float32),
        ],
        compiler_params=vmem_params(),
        cost_estimate=pl.CostEstimate(
            flops=36 * rows * edits * edits, bytes_accessed=16 * rows * edits, transcendentals=0
        ),
    )(*operands)


def sum_all(block, rows, cols):
    total = rows * cols
    me = lax.axis_index("row") * cols + lax.axis_index("col")
    strides = bits_of(total, 1)
    for stride in strides:
        pairs = [(i, i ^ stride) for i in range(total)]
        size = block.shape[0] // 2
        digit = (me // stride) % 2
        got = send(lax.dynamic_slice_in_dim(block, (1 - digit) * size, size, 0), pairs)
        block = lax.dynamic_slice_in_dim(block, digit * size, size, 0) + got
    for stride in reversed(strides):
        pairs = [(i, i ^ stride) for i in range(total)]
        digit = (me // stride) % 2
        got = send(block, pairs)
        block = jnp.concatenate([jnp.where(digit == 0, block, got), jnp.where(digit == 0, got, block)])
    return block


def squared_norm(matrix):
    return jnp.sum(matrix * matrix)


def scaled_error(matrix, scale_ref, error_ref):
    order = matrix.shape[0]
    row = lax.broadcasted_iota(jnp.int32, (order, order), 0)
    col = lax.broadcasted_iota(jnp.int32, (order, order), 1)
    eye = jnp.where(row == col, 1.0, 0.0).astype(jnp.float32)
    diagonal = matrix * eye
    across = lax.rsqrt(jnp.sum(diagonal, axis=0, keepdims=True))
    down = lax.rsqrt(jnp.sum(diagonal, axis=1, keepdims=True))
    scale_ref[...] = down
    unit = matrix * across * down
    error = eye - unit
    square = dot(error, error)
    safe = squared_norm(square) < 0.9
    bound = jnp.max(jnp.sum(jnp.abs(unit), axis=1))
    factor = jnp.where(safe, 1.0, 1.0 / bound)
    error_ref[...] = eye - factor * unit
    return factor


def power_solve(matrix, rhs, scale_ref, error_ref, value_ref):
    factor = scaled_error(matrix, scale_ref, error_ref)
    value_ref[...] = factor * scale_ref[...] * rhs

    def step(state):
        count, _ = state
        error = error_ref[...]
        value_ref[...] += dot(error, value_ref[...])
        size = squared_norm(error)
        error_ref[...] = dot(error, error)
        return count + 1, size

    lax.while_loop(lambda s: (s[0] < MAX_SQUARINGS) & (s[1] > DONE), step, (0, jnp.float32(1.0)))
    return scale_ref[...] * value_ref[...]


def solve_kernel(first, grams, norm_in, alpha, beta, norm_out, scale, error, value):
    order = alpha.shape[0]
    square = grams[0:order]
    cross = grams[order : 2 * order]
    norm = grams[2 * order :] if first else norm_in[...]
    curvature = cross if first else grams[2 * order :]
    curvature = 0.5 * (curvature + curvature.T)
    step = power_solve(curvature, norm, scale, error, value)
    alpha[...] = step
    change = dot(step.T, dot(square, step) - 2.0 * cross)
    after = norm + 0.5 * (change + change.T)
    norm_out[...] = after
    beta[...] = power_solve(norm, after, scale, error, value)


def solve_small(grams, norm, first):
    edits = grams.shape[1]
    square = jax.ShapeDtypeStruct((edits, edits), jnp.float32)
    return pl.pallas_call(
        functools.partial(solve_kernel, first),
        out_shape=[square, square, square],
        scratch_shapes=[
            pltpu.VMEM((edits, 1), jnp.float32),
            pltpu.VMEM((edits, edits), jnp.float32),
            pltpu.VMEM((edits, edits), jnp.float32),
        ],
        compiler_params=vmem_params(),
        cost_estimate=pl.CostEstimate(
            flops=200 * edits * edits * edits, bytes_accessed=32 * edits * edits, transcendentals=0
        ),
    )(grams, norm)


def update_kernel(residual, direction, image, alpha, beta, residual_out, direction_out, lowered_out):
    after = residual[...] - dot(image[...], alpha[...])
    residual_out[...] = after
    following = after + dot(direction[...], beta[...])
    direction_out[...] = following
    lowered_out[...] = following.astype(jnp.bfloat16)


def update(residual, direction, image, alpha, beta):
    rows, edits = residual.shape
    full = jax.ShapeDtypeStruct((rows, edits), jnp.float32)
    return pl.pallas_call(
        update_kernel,
        out_shape=[full, full, jax.ShapeDtypeStruct((rows, edits), jnp.bfloat16)],
        compiler_params=vmem_params(),
        cost_estimate=pl.CostEstimate(
            flops=24 * rows * edits * edits, bytes_accessed=22 * rows * edits, transcendentals=0
        ),
    )(residual, direction, image, alpha, beta)


def body(rows, cols, covariance, right_side):
    order = ring_order(rows)
    to_outer = [(k, (k % rows) * cols + k // rows) for k in range(rows * cols)]
    to_inner = [(b, a) for a, b in to_outer]
    residual = direction = right_side
    inner_residual = inner_direction = send(right_side, to_inner)
    lowered = right_side.astype(jnp.bfloat16)
    iterate = norm = None
    for iteration in range(ITERS):
        first, last = iteration == 0, iteration == ITERS - 1
        total = partial_image(covariance, lowered, order, cols)
        own, got = exchange_sum(total, cols)
        inner_image, grams = local_grams(own, got, inner_residual, inner_direction, first)
        image = send(inner_image, to_outer)
        grams = sum_all(grams, rows, cols)
        alpha, beta, norm = solve_small(grams, grams[: grams.shape[1]] if first else norm, first)
        moved = dot(direction, alpha)
        iterate = moved if first else iterate + moved
        residual, direction, lowered = update(residual, direction, image, alpha, beta)
        if not last:
            inner_residual, inner_direction, _ = update(
                inner_residual, inner_direction, inner_image, alpha, beta
            )
    return (iterate, residual, direction)


def solution(mesh):
    place = P(("col", "row"), None)
    return jax.shard_map(
        functools.partial(body, mesh.shape["row"], mesh.shape["col"]),
        mesh=mesh,
        in_specs=(P("row", "col"), place),
        out_specs=(place, place, place),
        check_vma=False,
    )
```

```python
import functools

import jax
import jax.numpy as jnp
import numpy as np
from jax import lax
from jax.experimental import pallas as pl
from jax.experimental.pallas import tpu as pltpu
from jax.sharding import PartitionSpec as P

ITERS = 3
AXES = ("row", "col")
HIGHEST = lax.Precision.HIGHEST
VMEM_LIMIT = 48 * 1024 * 1024
DONE = 3e-8
MAX_SQUARINGS = 48


def dot(left, right):
    return jnp.dot(left, right, precision=HIGHEST, preferred_element_type=jnp.float32)


def send(block, pairs):
    return lax.ppermute(block, AXES, pairs)


def vmem_params(**extra):
    return pltpu.CompilerParams(vmem_limit_bytes=VMEM_LIMIT, **extra)


def bits_of(size, first_stride):
    assert size & (size - 1) == 0
    return [first_stride << b for b in range(size.bit_length() - 1)]


def ring_order(rows):
    fast = 1 << ((rows.bit_length() - 1) // 2)
    slow = rows // fast
    if fast == 1 or slow == 1:
        return list(range(rows))
    cycle = [s * fast for s in range(slow)]
    for s in reversed(range(slow)):
        lane = range(1, fast) if (slow - 1 - s) % 2 == 0 else reversed(range(1, fast))
        cycle += [s * fast + f for f in lane]
    return cycle


def index_table(order, cols):
    rows = len(order)
    place = {r: i for i, r in enumerate(order)}
    shifts = [0] + [s for d in range(1, rows // 2) for s in (-d, d)] + [rows // 2]
    return np.array(
        [
            [c ^ j for j in range(cols)] + [order[(place[r] + s) % rows] for s in shifts]
            for r in range(rows)
            for c in range(cols)
        ],
        np.int32,
    )


def chunk_kernel(blocks, has_base, index_ref, *refs):
    covs, parts = refs[:blocks], refs[blocks : 2 * blocks]
    out = refs[-1]
    total = refs[2 * blocks][...] if has_base else None
    for cov, part in zip(covs, parts):
        term = jnp.dot(cov[...], part[...], preferred_element_type=jnp.float32)
        total = term if total is None else total + term
    out[...] = total


def add_chunks(covariance, index, cols, first_owner, parts, base, begin, count):
    blocks = len(parts)
    depth, edits = parts[0].shape
    height = covariance.shape[0] // cols
    has_base = base is not None

    def cov_spec(t):
        return pl.BlockSpec((height, depth), lambda i, ix: (ix[begin + i], ix[cols + first_owner + t]))

    part_specs = [pl.BlockSpec((depth, edits), lambda i, ix: (0, 0)) for _ in parts]
    base_spec = [pl.BlockSpec((height, edits), lambda i, ix: (begin + i, 0))] if has_base else []
    operands = [covariance] * blocks + list(parts) + ([base] if has_base else [])
    whole = has_base and count == cols
    return pl.pallas_call(
        functools.partial(chunk_kernel, blocks, has_base),
        grid_spec=pltpu.PrefetchScalarGridSpec(
            num_scalar_prefetch=1,
            grid=(count,),
            in_specs=[cov_spec(t) for t in range(blocks)] + part_specs + base_spec,
            out_specs=pl.BlockSpec((height, edits), lambda i, ix: (i, 0)),
        ),
        out_shape=jax.ShapeDtypeStruct((count * height, edits), jnp.float32),
        input_output_aliases={1 + 2 * blocks: 0} if whole else {},
        compiler_params=vmem_params(),
        cost_estimate=pl.CostEstimate(
            flops=2 * count * height * depth * blocks * edits,
            bytes_accessed=2 * count * height * depth * blocks,
            transcendentals=0,
        ),
    )(index, *operands)


def partial_image(covariance, lowered, order, index, cols, aside):
    rows = len(order)
    depth = lowered.shape[0]
    quarter = covariance.shape[0] // cols
    if depth % 128 or depth % 32 or quarter % 16 or rows % 2:
        whole = lax.all_gather(lowered, "row", axis=0, tiled=True)
        product = jnp.dot(covariance, whole, preferred_element_type=jnp.float32)
        swapped = product.reshape(cols, quarter, -1)[index[:cols]]
        return [swapped[j] for j in range(cols)], aside
    following = {order[i]: order[(i + 1) % rows] for i in range(rows)}
    forward = [(r * cols + c, following[r] * cols + c) for r in range(rows) for c in range(cols)]
    backward = [(b, a) for a, b in forward]
    half = depth // 2
    ahead = behind = lowered
    held, owner, total = [lowered], 0, None
    for step in range(1, rows // 2 + 1):
        if step < rows // 2:
            behind, ahead = send(behind, forward), send(ahead, backward)
            arrived = [behind, ahead]
        else:
            arrived = [jnp.concatenate([send(behind[:half], forward), send(ahead[half:], backward)])]
        total = add_chunks(covariance, index, cols, owner, held, total, 0, cols)
        owner += len(held)
        if step < rows // 2:
            if step == 2:
                total, aside = lax.optimization_barrier((total, aside))
            total, behind, ahead = lax.optimization_barrier((total, behind, ahead))
            arrived = [behind, ahead]
        held = arrived
    upper = add_chunks(covariance, index, cols, owner, held, total, cols // 2, cols // 2)
    lower = add_chunks(covariance, index, cols, owner, held, total, 0, cols // 2)
    return [part[j * quarter : (j + 1) * quarter] for part in (lower, upper) for j in range(cols // 2)], aside


def exchange_sum(pieces, rows):
    cols = len(pieces)
    pieces = dict(enumerate(pieces))
    strides = bits_of(cols, 1)
    for bit in strides:
        pairs = [(i, i ^ bit) for i in range(rows * cols)]
        got = {}
        for j in sorted((j for j in pieces if j & bit), reverse=True):
            block = pieces[j].astype(jnp.bfloat16) if bit > 1 else pieces[j]
            got[j ^ bit] = send(block, pairs)
        if bit == strides[-1]:
            return pieces[0], got[0]
        pieces = {j: pieces[j] + got[j].astype(jnp.float32) for j in got}


def gram_kernel(first, own, got, residual, *refs):
    direction = None if first else refs[0]
    image, grams = refs[-2:]
    image[...] = (own[...] + got[...].astype(jnp.float32)).astype(jnp.bfloat16)
    value = image[...].astype(jnp.float32)
    order = value.shape[1]
    flipped = value.T
    grams[0:order] = dot(flipped, value)
    grams[order : 2 * order] = dot(flipped, residual[...])
    if first:
        grams[2 * order :] = dot(residual[...].T, residual[...])
    else:
        grams[2 * order :] = dot(flipped, direction[...])


def local_grams(own, got, residual, direction, first):
    rows, edits = own.shape
    operands = [own, got, residual] + ([] if first else [direction])
    return pl.pallas_call(
        functools.partial(gram_kernel, first),
        out_shape=[
            jax.ShapeDtypeStruct((rows, edits), jnp.bfloat16),
            jax.ShapeDtypeStruct((3 * edits, edits), jnp.float32),
        ],
        compiler_params=vmem_params(),
        cost_estimate=pl.CostEstimate(
            flops=36 * rows * edits * edits, bytes_accessed=16 * rows * edits, transcendentals=0
        ),
    )(*operands)


def partners(total, stride, size, step):
    return [(i, i + (((i // stride) % size ^ step) - (i // stride) % size) * stride) for i in range(total)]


def sum_all(block, rows, cols, rider, hops):
    total = rows * cols
    me = lax.axis_index("row") * cols + lax.axis_index("col")
    plane = cols // 2 * min(2, rows)
    scatter = [(1, 2), (2, plane)]
    exchange = [(stride, 2) for stride in bits_of(total // (2 * plane), 2 * plane)]
    for stride, size in scatter:
        digit = (me // stride) % size
        piece = block.shape[0] // size
        got = [
            send(lax.dynamic_slice_in_dim(block, (digit ^ step) * piece, piece, 0), partners(total, stride, size, step))
            for step in range(1, size)
        ]
        block = lax.dynamic_slice_in_dim(block, digit * piece, piece, 0)
        for term in got:
            block = block + term
    block, rider = lax.optimization_barrier((block, rider))
    rider = send(rider, hops[0])
    for stride, _ in exchange:
        block = block + send(block, partners(total, stride, 2, 1))
    block, rider = lax.optimization_barrier((block, rider))
    rider = send(rider, hops[1])
    for stride, size in reversed(scatter):
        digit = (me // stride) % size
        piece = block.shape[0]
        whole = jnp.zeros((size * piece,) + block.shape[1:], block.dtype)
        for step in range(size):
            part = send(block, partners(total, stride, size, step)) if step else block
            whole = lax.dynamic_update_slice_in_dim(whole, part, (digit ^ step) * piece, 0)
        block = whole
    return block, rider


def squared_norm(matrix):
    return jnp.sum(matrix * matrix)


def power_solve(matrix, rhs, scale_ref, error_ref, value_ref):
    order = matrix.shape[0]
    row = lax.broadcasted_iota(jnp.int32, (order, order), 0)
    col = lax.broadcasted_iota(jnp.int32, (order, order), 1)
    eye = jnp.where(row == col, 1.0, 0.0).astype(jnp.float32)
    diagonal = matrix * eye
    across = lax.rsqrt(jnp.sum(diagonal, axis=0, keepdims=True))
    scale_ref[...] = lax.rsqrt(jnp.sum(diagonal, axis=1, keepdims=True))
    unit = matrix * across * scale_ref[...]
    error = eye - unit
    square = dot(error, error)
    size = squared_norm(square)
    safe = size < 0.9
    start = scale_ref[...] * (eye if rhs is None else rhs)

    @pl.when(safe)
    def _():
        value_ref[...] = start + dot(error, start)
        error_ref[...] = square

    @pl.when(jnp.logical_not(safe))
    def _():
        factor = 1.0 / jnp.max(jnp.sum(jnp.abs(unit), axis=1))
        value_ref[...] = factor * start
        error_ref[...] = eye - factor * unit

    def step(state):
        count, _ = state
        error = error_ref[...]
        value_ref[...] += dot(error, value_ref[...])
        error_ref[...] = dot(error, error)
        return count + 1, squared_norm(error)

    lax.while_loop(lambda s: (s[0] < MAX_SQUARINGS) & (s[1] > DONE), step, (0, jnp.float32(1.0)))
    return scale_ref[...] * value_ref[...]


def solve_kernel(first, grams, *refs):
    alpha, beta, norm_out, scale, error, value = refs[-6:]
    order = alpha.shape[0]
    square = grams[0:order]
    cross = grams[order : 2 * order]
    norm = grams[2 * order :] if first else refs[0][...]
    curvature = cross if first else grams[2 * order :]
    curvature = 0.5 * (curvature + curvature.T)
    step = power_solve(curvature, norm, scale, error, value)
    alpha[...] = step
    change = dot(step.T, dot(square, step) - 2.0 * cross)
    after = norm + 0.5 * (change + change.T)
    norm_out[...] = after
    beta[...] = power_solve(norm, after, scale, error, value) if first else dot(refs[1][...], after)


def small_scratch(edits):
    return [
        pltpu.VMEM((edits, 1), jnp.float32),
        pltpu.VMEM((edits, edits), jnp.float32),
        pltpu.VMEM((edits, edits), jnp.float32),
    ]


def solve_small(grams, norm, inverse):
    edits = grams.shape[1]
    square = jax.ShapeDtypeStruct((edits, edits), jnp.float32)
    return pl.pallas_call(
        functools.partial(solve_kernel, norm is None),
        out_shape=[square, square, square],
        scratch_shapes=small_scratch(edits),
        compiler_params=vmem_params(),
        cost_estimate=pl.CostEstimate(
            flops=100 * edits * edits * edits, bytes_accessed=32 * edits * edits, transcendentals=0
        ),
    )(grams, *([] if norm is None else [norm, inverse]))


def inverse_kernel(matrix, out, scale, error, value):
    out[...] = power_solve(matrix[...], None, scale, error, value)


def inverse_small(matrix):
    edits = matrix.shape[0]
    return pl.pallas_call(
        inverse_kernel,
        out_shape=jax.ShapeDtypeStruct((edits, edits), jnp.float32),
        scratch_shapes=small_scratch(edits),
        compiler_params=vmem_params(),
        cost_estimate=pl.CostEstimate(
            flops=100 * edits * edits * edits, bytes_accessed=8 * edits * edits, transcendentals=0
        ),
    )(matrix)


def update_kernel(residual, direction, image, alpha, beta, residual_out, direction_out, lowered_out):
    after = residual[...] - dot(image[...].astype(jnp.float32), alpha[...])
    residual_out[...] = after
    following = after + dot(direction[...], beta[...])
    direction_out[...] = following
    lowered_out[...] = following.astype(jnp.bfloat16)


def update(residual, direction, image, alpha, beta):
    rows, edits = residual.shape
    full = jax.ShapeDtypeStruct((rows, edits), jnp.float32)
    return pl.pallas_call(
        update_kernel,
        out_shape=[full, full, jax.ShapeDtypeStruct((rows, edits), jnp.bfloat16)],
        compiler_params=vmem_params(),
        cost_estimate=pl.CostEstimate(
            flops=24 * rows * edits * edits, bytes_accessed=22 * rows * edits, transcendentals=0
        ),
    )(residual, direction, image, alpha, beta)


def advance_kernel(iterate, direction, alpha, out):
    out[...] = iterate[...] + dot(direction[...], alpha[...])


def start_kernel(direction, alpha, out):
    out[...] = dot(direction[...], alpha[...])


def advance(iterate, direction, alpha):
    rows, edits = direction.shape
    return pl.pallas_call(
        start_kernel if iterate is None else advance_kernel,
        out_shape=jax.ShapeDtypeStruct((rows, edits), jnp.float32),
        compiler_params=vmem_params(),
        cost_estimate=pl.CostEstimate(
            flops=12 * rows * edits * edits, bytes_accessed=12 * rows * edits, transcendentals=0
        ),
    )(*([] if iterate is None else [iterate]), direction, alpha)


def body(rows, cols, covariance, right_side):
    total = rows * cols
    order = ring_order(rows)
    me = lax.axis_index("row") * cols + lax.axis_index("col")
    table = index_table(order, cols)
    index = lax.dynamic_index_in_dim(jnp.asarray(table), me, 0, keepdims=False)
    to_outer = {k: (k % rows) * cols + k // rows for k in range(total)}
    swap = {k: k ^ (cols + 1) if (k // cols ^ k) & 1 else k for k in range(total)}
    hops = [list(swap.items()), [(swap[k], to_outer[k]) for k in range(total)]]
    residual = direction = right_side
    inner_residual = inner_direction = send(right_side, [(b, a) for a, b in to_outer.items()])
    lowered = right_side.astype(jnp.bfloat16)
    iterate = norm = inverse = alpha = earlier = None
    for iteration in range(ITERS):
        first, last = iteration == 0, iteration == ITERS - 1
        aside = () if first else (inverse_small(norm), advance(iterate, earlier, alpha))
        pieces, aside = partial_image(covariance, lowered, order, index, cols, aside)
        if not first:
            inverse, iterate = aside
        own, got = exchange_sum(pieces, rows)
        inner_image, grams = local_grams(own, got, inner_residual, inner_direction, first)
        grams, image = sum_all(grams, rows, cols, inner_image, hops)
        alpha, beta, norm = solve_small(grams, norm, inverse)
        earlier = direction
        residual, direction, lowered = update(residual, direction, image, alpha, beta)
        if not last:
            inner_residual, inner_direction, _ = update(
                inner_residual, inner_direction, inner_image, alpha, beta
            )
    return (advance(iterate, earlier, alpha), residual, direction)


def solution(mesh):
    place = P(("col", "row"), None)
    return jax.shard_map(
        functools.partial(body, mesh.shape["row"], mesh.shape["col"]),
        mesh=mesh,
        in_specs=(P("row", "col"), place),
        out_specs=(place, place, place),
        check_vma=False,
    )
```

```python
import functools

import jax
import jax.numpy as jnp
import numpy as np
from jax import lax
from jax.experimental import pallas as pl
from jax.experimental.pallas import tpu as pltpu
from jax.sharding import PartitionSpec as P

ITERS = 3
AXES = ("row", "col")
HIGHEST = lax.Precision.HIGHEST
VMEM_LIMIT = 14 * 1024 * 1024
SLOTS = 3
DONE = 3e-8
MAX_SQUARINGS = 48


def dot(left, right):
    return jnp.dot(left, right, precision=HIGHEST, preferred_element_type=jnp.float32)


def dot_parts(left, right):
    total = None
    for _ in range(3):
        part = right.astype(jnp.bfloat16)
        right = right - part.astype(jnp.float32)
        term = jnp.dot(left, part, preferred_element_type=jnp.float32)
        total = term if total is None else total + term
    return total


def send(block, pairs):
    return lax.ppermute(block, AXES, pairs)


def vmem_params(**extra):
    return pltpu.CompilerParams(vmem_limit_bytes=VMEM_LIMIT, **extra)


def bits_of(size, first_stride):
    assert size & (size - 1) == 0
    return [first_stride << b for b in range(size.bit_length() - 1)]


def ring_order(rows):
    fast = 1 << ((rows.bit_length() - 1) // 2)
    slow = rows // fast
    if fast == 1 or slow == 1:
        return list(range(rows))
    cycle = [s * fast for s in range(slow)]
    for s in reversed(range(slow)):
        lane = range(1, fast) if (slow - 1 - s) % 2 == 0 else reversed(range(1, fast))
        cycle += [s * fast + f for f in lane]
    return cycle


def quarter_of(row, col, cols):
    return col ^ ((row >> 1 & 1) * min(2, cols // 2))


def index_table(order, cols):
    rows = len(order)
    place = {r: i for i, r in enumerate(order)}
    shifts = [0] + [s for d in range(1, rows // 2) for s in (-d, d)] + [rows // 2]
    return np.array(
        [
            [quarter_of(r, c ^ j, cols) for j in range(cols)] + [order[(place[r] + s) % rows] for s in shifts]
            for r in range(rows)
            for c in range(cols)
        ],
        np.int32,
    )


def chunk_kernel(blocks, halves, has_base, cols, first_owner, begin, count, index, cov, *refs):
    parts = refs[: blocks * halves]
    base = refs[blocks * halves] if has_base else None
    out, tiles, arrived, joined = refs[-4:]
    piece = parts[0].shape[0]
    depth = piece * halves
    height = tiles.shape[1]

    def fetch(step, t):
        slot = lax.rem(step, SLOTS)
        row = pl.multiple_of(index[begin + step] * height, 16)
        col = pl.multiple_of(index[cols + first_owner + t] * depth, 128)
        return pltpu.make_async_copy(
            cov.at[pl.ds(row, height), pl.ds(col, depth)],
            tiles.at[slot, :, pl.ds(t * depth, depth)],
            arrived.at[slot, t],
        )

    for step in range(min(SLOTS - 1, count)):
        for t in range(blocks):
            fetch(jnp.int32(step), t).start()
    for at, part in enumerate(parts):
        joined[at * piece : (at + 1) * piece, :] = part[...]

    def one(step, carry):
        @pl.when(step + SLOTS - 1 < count)
        def _():
            for t in range(blocks):
                fetch(step + SLOTS - 1, t).start()

        for t in range(blocks):
            fetch(step, t).wait()
        slot = lax.rem(step, SLOTS)
        term = jnp.dot(tiles[slot], joined[...], preferred_element_type=jnp.float32)
        if has_base:
            term = term + base[pl.ds(pl.multiple_of((begin + step) * height, 16), height), :]
        out[pl.ds(pl.multiple_of(step * height, 16), height), :] = term
        return carry

    lax.fori_loop(0, count, one, 0)


def add_chunks(covariance, index, cols, first_owner, parts, halves, base, begin, count):
    blocks = len(parts) // halves
    piece, edits = parts[0].shape
    depth = piece * halves
    height = covariance.shape[0] // cols
    has_base = base is not None
    operands = [index, covariance] + list(parts) + ([base] if has_base else [])
    in_vmem = pl.BlockSpec(memory_space=pltpu.VMEM)
    return pl.pallas_call(
        functools.partial(chunk_kernel, blocks, halves, has_base, cols, first_owner, begin, count),
        in_specs=[pl.BlockSpec(memory_space=pltpu.SMEM), pl.BlockSpec(memory_space=pl.ANY)]
        + [in_vmem] * (len(operands) - 2),
        out_specs=in_vmem,
        out_shape=jax.ShapeDtypeStruct((count * height, edits), jnp.float32),
        scratch_shapes=[
            pltpu.VMEM((SLOTS, height, blocks * depth), jnp.bfloat16),
            pltpu.SemaphoreType.DMA((SLOTS, blocks)),
            pltpu.VMEM((blocks * depth, edits), jnp.bfloat16),
        ],
        input_output_aliases={len(operands) - 1: 0} if has_base and count == cols else {},
        compiler_params=vmem_params(),
        cost_estimate=pl.CostEstimate(
            flops=2 * count * height * depth * blocks * edits,
            bytes_accessed=2 * count * height * depth * blocks,
            transcendentals=0,
        ),
    )(*operands)


def partial_image(covariance, lowered, order, index, cols, rider, hops):
    rows = len(order)
    depth = lowered.shape[0]
    quarter = covariance.shape[0] // cols
    if depth % 128 or depth % 32 or quarter % 16 or rows % 2:
        whole = lax.all_gather(lowered, "row", axis=0, tiled=True)
        product = jnp.dot(covariance, whole, preferred_element_type=jnp.float32)
        swapped = product.reshape(cols, quarter, -1)[index[:cols]]
        for pairs in hops:
            rider = send(rider, pairs)
        return [swapped[j] for j in range(cols)], rider
    following = {order[i]: order[(i + 1) % rows] for i in range(rows)}
    forward = [(r * cols + c, following[r] * cols + c) for r in range(rows) for c in range(cols)]
    backward = [(b, a) for a, b in forward]
    half = depth // 2
    behind = ahead = [lowered[:half], lowered[half:]]
    held, owner, total = behind, 0, None
    for step in range(1, rows // 2 + 1):
        if step < rows // 2:
            pairs = [(send(low, forward), send(high, backward)) for low, high in zip(behind, ahead)]
            behind, ahead = zip(*pairs)
            arrived = list(behind) + list(ahead)
        else:
            arrived = [send(behind[0], forward), send(ahead[1], backward)]
        total = add_chunks(covariance, index, cols, owner, held, 2, total, 0, cols)
        owner += len(held) // 2
        if step < rows // 2:
            if step > 1 and len(hops) >= step - 1:
                rider = send(rider, hops[step - 2])
                if step > 2:
                    total, rider = lax.optimization_barrier((total, rider))
            total, low, high = lax.optimization_barrier((total, behind[0], ahead[0]))
            behind, ahead = [low, behind[1]], [high, ahead[1]]
            arrived = behind + ahead
        held = arrived
    upper = add_chunks(covariance, index, cols, owner, held, 2, total, cols // 2, cols // 2)
    lower = add_chunks(covariance, index, cols, owner, held, 2, total, 0, cols // 2)
    return [part[j * quarter : (j + 1) * quarter] for part in (lower, upper) for j in range(cols // 2)], rider


def exchange_sum(pieces, rows):
    cols = len(pieces)
    pieces = dict(enumerate(pieces))
    strides = bits_of(cols, 1)
    for bit in strides:
        pairs = [(i, i ^ bit) for i in range(rows * cols)]
        got = {}
        for j in sorted((j for j in pieces if j & bit), reverse=True):
            block = pieces[j].astype(jnp.bfloat16) if bit > 1 else pieces[j]
            got[j ^ bit] = send(block, pairs)
        if bit == strides[-1]:
            return pieces[0], got[0]
        pieces = {j: pieces[j] + got[j].astype(jnp.float32) for j in got}


def norm_kernel(residual, out):
    value = residual[...]
    out[...] = dot(value.T, value)


def local_norm(residual):
    rows, edits = residual.shape
    return pl.pallas_call(
        norm_kernel,
        out_shape=jax.ShapeDtypeStruct((edits, edits), jnp.float32),
        compiler_params=vmem_params(),
        cost_estimate=pl.CostEstimate(
            flops=12 * rows * edits * edits, bytes_accessed=4 * rows * edits, transcendentals=0
        ),
    )(residual)


def square_index(order):
    shape = (order, order)
    return lax.broadcasted_iota(jnp.int32, shape, 0), lax.broadcasted_iota(jnp.int32, shape, 1)


def pack(norm, square, curvature):
    row, col = square_index(norm.shape[0])
    diagonal = jnp.sum(jnp.where(row == col, square, 0.0), axis=1, keepdims=True)
    below = jnp.where(col == 0, diagonal, diagonal[0:1, 0:1])
    return jnp.where(col >= row, norm, below), jnp.where(col >= row, curvature, square)


def unpack(with_norm, with_curvature):
    row, col = square_index(with_norm.shape[0])

    def mirror(half, diagonal):
        return jnp.where(row == col, diagonal, half + half.T)

    norm = mirror(jnp.where(col > row, with_norm, 0.0), with_norm)
    curvature = mirror(jnp.where(col > row, with_curvature, 0.0), with_curvature)
    diagonal = jnp.where(row == 0, with_norm[2:3, 1:2], with_norm[:, 0:1])
    return norm, mirror(jnp.where(col < row, with_curvature, 0.0), diagonal), curvature


def gram_kernel(own, got, norm, *refs):
    image, grams = refs[-2:]
    value = (own[...] + got[...].astype(jnp.float32)).astype(jnp.bfloat16)
    image[...] = value
    order = value.shape[1]
    flipped = value.T
    square = jnp.dot(flipped, value, preferred_element_type=jnp.float32)
    cross = dot_parts(flipped, refs[0][...])
    if len(refs) == 3:
        grams[0:order], grams[order : 2 * order] = norm[...], square
    else:
        curvature = dot_parts(flipped, refs[1][...])
        curvature = 0.5 * (curvature + curvature.T)
        grams[0:order], grams[order : 2 * order] = pack(norm[...], square, curvature)
    grams[2 * order :] = cross


def local_grams(own, got, norm, blocks):
    rows, edits = own.shape
    return pl.pallas_call(
        gram_kernel,
        out_shape=[
            jax.ShapeDtypeStruct((rows, edits), jnp.bfloat16),
            jax.ShapeDtypeStruct((3 * edits, edits), jnp.float32),
        ],
        compiler_params=vmem_params(),
        cost_estimate=pl.CostEstimate(
            flops=14 * rows * edits * edits, bytes_accessed=16 * rows * edits, transcendentals=0
        ),
    )(own, got, norm, *blocks)


def partners(total, stride, size, step):
    return [(i, i + (((i // stride) % size ^ step) - (i // stride) % size) * stride) for i in range(total)]


def sum_all(block, rows, cols, rider, hops):
    total = rows * cols
    me = lax.axis_index("row") * cols + lax.axis_index("col")
    plane = cols // 2 * min(2, rows)
    scatter = [(1, 2), (2, plane)]
    exchange = [(stride, 2) for stride in bits_of(total // (2 * plane), 2 * plane)]
    for stride, size in scatter:
        digit = (me // stride) % size
        piece = block.shape[0] // size
        got = [
            send(lax.dynamic_slice_in_dim(block, (digit ^ step) * piece, piece, 0), partners(total, stride, size, step))
            for step in range(1, size)
        ]
        block = lax.dynamic_slice_in_dim(block, digit * piece, piece, 0)
        for term in got:
            block = block + term
    block, rider = lax.optimization_barrier((block, rider))
    rider = send(rider, hops[0])
    for stride, _ in exchange:
        block = block + send(block, partners(total, stride, 2, 1))
    block, rider = lax.optimization_barrier((block, rider))
    rider = send(rider, hops[1])
    for stride, size in reversed(scatter):
        digit = (me // stride) % size
        piece = block.shape[0]
        whole = jnp.zeros((size * piece,) + block.shape[1:], block.dtype)
        for step in range(size):
            part = send(block, partners(total, stride, size, step)) if step else block
            whole = lax.dynamic_update_slice_in_dim(whole, part, (digit ^ step) * piece, 0)
        block = whole
    return block, rider


def squared_norm(matrix):
    return jnp.sum(matrix * matrix)


def power_solve(matrix, rhs, scale_ref, error_ref, value_ref):
    order = matrix.shape[0]
    row = lax.broadcasted_iota(jnp.int32, (order, order), 0)
    col = lax.broadcasted_iota(jnp.int32, (order, order), 1)
    eye = jnp.where(row == col, 1.0, 0.0).astype(jnp.float32)
    diagonal = matrix * eye
    across = lax.rsqrt(jnp.sum(diagonal, axis=0, keepdims=True))
    scale_ref[...] = lax.rsqrt(jnp.sum(diagonal, axis=1, keepdims=True))
    unit = matrix * across * scale_ref[...]
    error = eye - unit
    square = dot(error, error)
    size = squared_norm(square)
    safe = size < 0.9
    start = scale_ref[...] * rhs

    @pl.when(safe)
    def _():
        value_ref[...] = start + dot(error, start)
        error_ref[...] = square

    @pl.when(jnp.logical_not(safe))
    def _():
        factor = 1.0 / jnp.max(jnp.sum(jnp.abs(unit), axis=1))
        value_ref[...] = factor * start
        error_ref[...] = eye - factor * unit

    def step(state):
        count, _ = state
        error = error_ref[...]
        value_ref[...] += dot(error, value_ref[...])
        error_ref[...] = dot(error, error)
        return count + 1, squared_norm(error)

    lax.while_loop(lambda s: (s[0] < MAX_SQUARINGS) & (s[1] > DONE), step, (0, jnp.float32(1.0)))
    return scale_ref[...] * value_ref[...]


def solve_kernel(first, grams, alpha, beta, scale, error, value):
    order = alpha.shape[0]
    norm, square, cross = (grams[at * order : (at + 1) * order] for at in range(3))
    if first:
        curvature = 0.5 * (cross + cross.T)
    else:
        norm, square, curvature = unpack(norm, square)
    step = power_solve(curvature, norm, scale, error, value)
    alpha[...] = step
    change = dot(step.T, dot(square, step) - 2.0 * cross)
    after = norm + 0.5 * (change + change.T)
    beta[...] = power_solve(norm, after, scale, error, value)


def solve_small(grams, first):
    edits = grams.shape[1]
    square = jax.ShapeDtypeStruct((edits, edits), jnp.float32)
    return pl.pallas_call(
        functools.partial(solve_kernel, first),
        out_shape=[square, square],
        scratch_shapes=[
            pltpu.VMEM((edits, 1), jnp.float32),
            pltpu.VMEM((edits, edits), jnp.float32),
            pltpu.VMEM((edits, edits), jnp.float32),
        ],
        compiler_params=vmem_params(),
        cost_estimate=pl.CostEstimate(flops=0, bytes_accessed=0, transcendentals=0),
    )(grams)


def update_kernel(residual, direction, image, alpha, beta, residual_out, direction_out, lowered_out):
    after = residual[...] - dot_parts(image[...], alpha[...])
    residual_out[...] = after
    following = after + dot(direction[...], beta[...])
    direction_out[...] = following
    lowered_out[...] = following.astype(jnp.bfloat16)


def update(residual, direction, image, alpha, beta):
    rows, edits = residual.shape
    full = jax.ShapeDtypeStruct((rows, edits), jnp.float32)
    return pl.pallas_call(
        update_kernel,
        out_shape=[full, full, jax.ShapeDtypeStruct((rows, edits), jnp.bfloat16)],
        compiler_params=vmem_params(),
        cost_estimate=pl.CostEstimate(
            flops=24 * rows * edits * edits, bytes_accessed=22 * rows * edits, transcendentals=0
        ),
    )(residual, direction, image, alpha, beta)


def advance_kernel(iterate, direction, alpha, out):
    out[...] = iterate[...] + dot(direction[...], alpha[...])


def start_kernel(direction, alpha, out):
    out[...] = dot(direction[...], alpha[...])


def advance(iterate, direction, alpha):
    rows, edits = direction.shape
    return pl.pallas_call(
        start_kernel if iterate is None else advance_kernel,
        out_shape=jax.ShapeDtypeStruct((rows, edits), jnp.float32),
        compiler_params=vmem_params(),
        cost_estimate=pl.CostEstimate(
            flops=12 * rows * edits * edits, bytes_accessed=12 * rows * edits, transcendentals=0
        ),
    )(*([] if iterate is None else [iterate]), direction, alpha)


def plane_hop(to_outer, swap, rows, cols):
    taken, plane = set(), {}
    for k in range(rows * cols):
        row, chip = to_outer[k] // cols, swap[k] % cols // 2
        place = next((row * cols + 2 * chip + core for core in (0, 1) if row * cols + 2 * chip + core not in taken), None)
        if place is None:
            return to_outer
        taken.add(place)
        plane[k] = place
    return plane


def body(rows, cols, covariance, right_side):
    total = rows * cols
    order = ring_order(rows)
    me = lax.axis_index("row") * cols + lax.axis_index("col")
    table = index_table(order, cols)
    index = lax.dynamic_index_in_dim(jnp.asarray(table), me, 0, keepdims=False)
    kept = {k: k // cols * cols + quarter_of(k // cols, k % cols, cols) for k in range(total)}
    to_outer = {k: (kept[k] % rows) * cols + kept[k] // rows for k in range(total)}
    swap = {k: k ^ (cols + 1) if (k // cols ^ k) & 1 else k for k in range(total)}
    hops = [list(swap.items()), [(swap[k], to_outer[k]) for k in range(total)]]
    plane = plane_hop(to_outer, swap, rows, cols)
    ways_in = [
        [(to_outer[k], plane[k]) for k in range(total)],
        [(plane[k], swap[k]) for k in range(total)],
        [(swap[k], k) for k in range(total)],
    ]
    residual = direction = right_side
    lowered = right_side.astype(jnp.bfloat16)
    inner_residual = inner_direction = None
    iterate = alpha = earlier = None
    for iteration in range(ITERS):
        first, last = iteration == 0, iteration == ITERS - 1
        pieces, inner = partial_image(
            covariance, lowered, order, index, cols, lowered if first else None, ways_in[:2] if first else []
        )
        own, got = exchange_sum(pieces, rows)
        norm = local_norm(residual)
        if first:
            own, norm, inner = lax.optimization_barrier((own, norm, inner))
            inner_residual = send(inner, ways_in[2]).astype(jnp.float32)
            blocks = [inner_residual]
            inner_direction = inner_residual
        else:
            iterate = advance(iterate, earlier, alpha)
            own, norm, iterate = lax.optimization_barrier((own, norm, iterate))
            blocks = [inner_residual, inner_direction]
        inner_image, grams = local_grams(own, got, norm, blocks)
        grams, image = sum_all(grams, rows, cols, inner_image, hops)
        alpha, beta = solve_small(grams, first)
        earlier = direction
        residual, direction, lowered = update(residual, direction, image, alpha, beta)
        if not last:
            inner_residual, inner_direction, _ = update(
                inner_residual, inner_direction, inner_image, alpha, beta
            )
    return (advance(iterate, earlier, alpha), residual, direction)


def solution(mesh):
    place = P(("col", "row"), None)
    return jax.shard_map(
        functools.partial(body, mesh.shape["row"], mesh.shape["col"]),
        mesh=mesh,
        in_specs=(P("row", "col"), place),
        out_specs=(place, place, place),
        check_vma=False,
    )
```

```python
import functools

import jax
import jax.numpy as jnp
import numpy as np
from jax import lax
from jax.experimental import pallas as pl
from jax.experimental.pallas import tpu as pltpu
from jax.sharding import PartitionSpec as P

ITERS = 3
AXES = ("row", "col")
HIGHEST = lax.Precision.HIGHEST
VMEM_LIMIT = 14 * 1024 * 1024
SLOTS = 3
DONE = 3e-8
MAX_SQUARINGS = 48


def dot(left, right):
    return jnp.dot(left, right, precision=HIGHEST, preferred_element_type=jnp.float32)


def dot_parts(left, right):
    total = None
    for _ in range(3):
        part = right.astype(jnp.bfloat16)
        right = right - part.astype(jnp.float32)
        term = jnp.dot(left, part, preferred_element_type=jnp.float32)
        total = term if total is None else total + term
    return total


def send(block, pairs):
    return lax.ppermute(block, AXES, pairs)


def vmem_params(**extra):
    return pltpu.CompilerParams(vmem_limit_bytes=VMEM_LIMIT, **extra)


def bits_of(size, first_stride):
    assert size & (size - 1) == 0
    return [first_stride << b for b in range(size.bit_length() - 1)]


def ring_order(rows):
    fast = 1 << ((rows.bit_length() - 1) // 2)
    slow = rows // fast
    if fast == 1 or slow == 1:
        return list(range(rows))
    cycle = [s * fast for s in range(slow)]
    for s in reversed(range(slow)):
        lane = range(1, fast) if (slow - 1 - s) % 2 == 0 else reversed(range(1, fast))
        cycle += [s * fast + f for f in lane]
    return cycle


def quarter_of(row, col, cols):
    return col ^ ((row >> 1 & 1) * min(2, cols // 2))


def ring_shifts(rows):
    return [0] + [s for d in range(1, rows // 2) for s in (-d, d)] + [rows // 2]


def index_table(order, cols):
    rows = len(order)
    place = {r: i for i, r in enumerate(order)}

    def line(r, c):
        quarters = [quarter_of(r, c ^ j, cols) for j in range(cols)]
        owners = [order[(place[r] + s) % rows] for s in ring_shifts(rows)]
        return quarters + owners + [owners.index((r * cols + q) % rows) for q in quarters]

    return np.array([line(r, c) for r in range(rows) for c in range(cols)], np.int32)


def pick_kernel(first, count, index, *refs):
    halves, outs = refs[:count], refs[count:]
    half = halves[0].shape[0]
    for j, out in enumerate(outs):
        for at in range(len(halves) // 2):

            @pl.when(index[first + j] == at)
            def _():
                out[0:half, :] = halves[2 * at][...]
                out[half : 2 * half, :] = halves[2 * at + 1][...]


def pick(index, halves, cols, first):
    half, edits = halves[0].shape
    return pl.pallas_call(
        functools.partial(pick_kernel, first, len(halves)),
        in_specs=[pl.BlockSpec(memory_space=pltpu.SMEM)] + [pl.BlockSpec(memory_space=pltpu.VMEM)] * len(halves),
        out_shape=[jax.ShapeDtypeStruct((2 * half, edits), halves[0].dtype)] * cols,
        compiler_params=vmem_params(),
        cost_estimate=pl.CostEstimate(flops=0, bytes_accessed=8 * half * edits * cols, transcendentals=0),
    )(index, *halves)


def spread(picked, rows, cols):
    holders = [r * cols // rows for r in range(rows)]
    kept = jnp.where(lax.axis_index("col") == lax.axis_index("row") * cols // rows, picked[0], jnp.zeros_like(picked[0]))
    return [kept] + [
        send(picked[j], [(r * cols + holders[r], r * cols + (holders[r] ^ j)) for r in range(rows)])
        for j in range(cols - 1, 0, -1)
    ]


def chunk_kernel(blocks, halves, has_base, cols, first_owner, begin, count, index, cov, *refs):
    parts = refs[: blocks * halves]
    base = refs[blocks * halves] if has_base else None
    out, tiles, arrived, joined = refs[-4:]
    piece = parts[0].shape[0]
    depth = piece * halves
    height = tiles.shape[1]

    def fetch(step, t):
        slot = lax.rem(step, SLOTS)
        row = pl.multiple_of(index[begin + step] * height, 16)
        col = pl.multiple_of(index[cols + first_owner + t] * depth, 128)
        return pltpu.make_async_copy(
            cov.at[pl.ds(row, height), pl.ds(col, depth)],
            tiles.at[slot, :, pl.ds(t * depth, depth)],
            arrived.at[slot, t],
        )

    for step in range(min(SLOTS - 1, count)):
        for t in range(blocks):
            fetch(jnp.int32(step), t).start()
    for at, part in enumerate(parts):
        joined[at * piece : (at + 1) * piece, :] = part[...]

    def one(step, carry):
        @pl.when(step + SLOTS - 1 < count)
        def _():
            for t in range(blocks):
                fetch(step + SLOTS - 1, t).start()

        for t in range(blocks):
            fetch(step, t).wait()
        slot = lax.rem(step, SLOTS)
        term = jnp.dot(tiles[slot], joined[...], preferred_element_type=jnp.float32)
        if has_base:
            term = term + base[pl.ds(pl.multiple_of((begin + step) * height, 16), height), :]
        out[pl.ds(pl.multiple_of(step * height, 16), height), :] = term
        return carry

    lax.fori_loop(0, count, one, 0)


def add_chunks(covariance, index, cols, first_owner, parts, halves, base, begin, count):
    blocks = len(parts) // halves
    piece, edits = parts[0].shape
    depth = piece * halves
    height = covariance.shape[0] // cols
    has_base = base is not None
    operands = [index, covariance] + list(parts) + ([base] if has_base else [])
    in_vmem = pl.BlockSpec(memory_space=pltpu.VMEM)
    return pl.pallas_call(
        functools.partial(chunk_kernel, blocks, halves, has_base, cols, first_owner, begin, count),
        in_specs=[pl.BlockSpec(memory_space=pltpu.SMEM), pl.BlockSpec(memory_space=pl.ANY)]
        + [in_vmem] * (len(operands) - 2),
        out_specs=in_vmem,
        out_shape=jax.ShapeDtypeStruct((count * height, edits), jnp.float32),
        scratch_shapes=[
            pltpu.VMEM((SLOTS, height, blocks * depth), jnp.bfloat16),
            pltpu.SemaphoreType.DMA((SLOTS, blocks)),
            pltpu.VMEM((blocks * depth, edits), jnp.bfloat16),
        ],
        input_output_aliases={len(operands) - 1: 0} if has_base and count == cols else {},
        compiler_params=vmem_params(),
        cost_estimate=pl.CostEstimate(
            flops=2 * count * height * depth * blocks * edits,
            bytes_accessed=2 * count * height * depth * blocks,
            transcendentals=0,
        ),
    )(*operands)


def partial_image(covariance, lowered, order, index, cols, first):
    rows = len(order)
    depth = lowered.shape[0]
    quarter = covariance.shape[0] // cols
    if depth % 128 or depth % 32 or quarter % 16 or rows % 2:
        whole = lax.all_gather(lowered, "row", axis=0, tiled=True)
        product = jnp.dot(covariance, whole, preferred_element_type=jnp.float32)
        swapped = product.reshape(cols, quarter, -1)[index[:cols]]
        inner = None
        if first:
            blocks = [
                lax.dynamic_slice_in_dim(whole, (lax.axis_index("row") * cols + index[j]) % rows * depth, depth, 0)
                for j in range(cols)
            ]
            inner = spread(blocks, rows, cols)
        return [swapped[j] for j in range(cols)], inner
    following = {order[i]: order[(i + 1) % rows] for i in range(rows)}
    forward = [(r * cols + c, following[r] * cols + c) for r in range(rows) for c in range(cols)]
    backward = [(b, a) for a, b in forward]
    half = depth // 2
    behind = ahead = [lowered[:half], lowered[half:]]
    held, owner, total = behind, 0, None
    seen = list(held)
    for step in range(1, rows // 2 + 1):
        if step < rows // 2:
            pairs = [(send(low, forward), send(high, backward)) for low, high in zip(behind, ahead)]
            behind, ahead = zip(*pairs)
            arrived = list(behind) + list(ahead)
        else:
            arrived = [send(behind[0], forward), send(ahead[1], backward)]
        total = add_chunks(covariance, index, cols, owner, held, 2, total, 0, cols)
        owner += len(held) // 2
        if step < rows // 2:
            total, low, high = lax.optimization_barrier((total, behind[0], ahead[0]))
            behind, ahead = [low, behind[1]], [high, ahead[1]]
            arrived = behind + ahead
        held = arrived
        seen += arrived
    inner = None
    if first:
        picked = pick(index, seen, cols, cols + rows)
        total, picked = lax.optimization_barrier((total, picked))
        inner = spread(picked, rows, cols)
    upper = add_chunks(covariance, index, cols, owner, held, 2, total, cols // 2, cols // 2)
    lower = add_chunks(covariance, index, cols, owner, held, 2, total, 0, cols // 2)
    return [part[j * quarter : (j + 1) * quarter] for part in (lower, upper) for j in range(cols // 2)], inner


def exchange_sum(pieces, rows, others):
    cols = len(pieces)
    far = cols // 2

    def fold(held):
        for bit in bits_of(far, 1):
            pairs = [(i, i ^ bit) for i in range(rows * cols)]
            got = {}
            for j in sorted((j for j in held if j & bit), reverse=True):
                block = held[j].astype(jnp.bfloat16) if bit > 1 else held[j]
                got[j ^ bit] = send(block, pairs)
            held = {j: held[j] + got[j].astype(jnp.float32) for j in got}
        return held

    leaving = fold({j: pieces[j] for j in range(far, cols)})[far].astype(jnp.bfloat16)
    leaving, others = lax.optimization_barrier((leaving, others))
    got = send(leaving, [(i, i ^ far) for i in range(rows * cols)])
    return fold(dict(enumerate(pieces[:far])))[0], got, others


def norm_kernel(residual, out):
    value = residual[...]
    out[...] = dot(value.T, value)


def local_norm(residual):
    rows, edits = residual.shape
    return pl.pallas_call(
        norm_kernel,
        out_shape=jax.ShapeDtypeStruct((edits, edits), jnp.float32),
        compiler_params=vmem_params(),
        cost_estimate=pl.CostEstimate(
            flops=12 * rows * edits * edits, bytes_accessed=4 * rows * edits, transcendentals=0
        ),
    )(residual)


def square_index(order):
    shape = (order, order)
    return lax.broadcasted_iota(jnp.int32, shape, 0), lax.broadcasted_iota(jnp.int32, shape, 1)


def pack(norm, square, curvature):
    row, col = square_index(norm.shape[0])
    diagonal = jnp.sum(jnp.where(row == col, square, 0.0), axis=1, keepdims=True)
    below = jnp.where(col == 0, diagonal, diagonal[0:1, 0:1])
    return jnp.where(col >= row, norm, below), jnp.where(col >= row, curvature, square)


def unpack(with_norm, with_curvature):
    row, col = square_index(with_norm.shape[0])

    def mirror(half, diagonal):
        return jnp.where(row == col, diagonal, half + half.T)

    norm = mirror(jnp.where(col > row, with_norm, 0.0), with_norm)
    curvature = mirror(jnp.where(col > row, with_curvature, 0.0), with_curvature)
    diagonal = jnp.where(row == 0, with_norm[2:3, 1:2], with_norm[:, 0:1])
    return norm, mirror(jnp.where(col < row, with_curvature, 0.0), diagonal), curvature


def gram_kernel(own, got, norm, *refs):
    image, grams = refs[-2:]
    value = (own[...] + got[...].astype(jnp.float32)).astype(jnp.bfloat16)
    image[...] = value
    order = value.shape[1]
    flipped = value.T
    square = jnp.dot(flipped, value, preferred_element_type=jnp.float32)
    cross = dot_parts(flipped, refs[0][...])
    if len(refs) == 3:
        grams[0:order], grams[order : 2 * order] = norm[...], square
    else:
        curvature = dot_parts(flipped, refs[1][...])
        curvature = 0.5 * (curvature + curvature.T)
        grams[0:order], grams[order : 2 * order] = pack(norm[...], square, curvature)
    grams[2 * order :] = cross


def local_grams(own, got, norm, blocks):
    rows, edits = own.shape
    return pl.pallas_call(
        gram_kernel,
        out_shape=[
            jax.ShapeDtypeStruct((rows, edits), jnp.bfloat16),
            jax.ShapeDtypeStruct((3 * edits, edits), jnp.float32),
        ],
        compiler_params=vmem_params(),
        cost_estimate=pl.CostEstimate(
            flops=14 * rows * edits * edits, bytes_accessed=16 * rows * edits, transcendentals=0
        ),
    )(own, got, norm, *blocks)


def partners(total, stride, size, step):
    return [(i, i + (((i // stride) % size ^ step) - (i // stride) % size) * stride) for i in range(total)]


def sum_all(block, rows, cols, rider, hops):
    total = rows * cols
    me = lax.axis_index("row") * cols + lax.axis_index("col")
    plane = cols // 2 * min(2, rows)
    scatter = [(1, 2), (2, plane)]
    exchange = [(stride, 2) for stride in bits_of(total // (2 * plane), 2 * plane)]
    for stride, size in scatter:
        digit = (me // stride) % size
        piece = block.shape[0] // size
        got = [
            send(lax.dynamic_slice_in_dim(block, (digit ^ step) * piece, piece, 0), partners(total, stride, size, step))
            for step in range(1, size)
        ]
        block = lax.dynamic_slice_in_dim(block, digit * piece, piece, 0)
        for term in got:
            block = block + term
    block, rider = lax.optimization_barrier((block, rider))
    rider = send(rider, hops[0])
    for stride, _ in exchange:
        block = block + send(block, partners(total, stride, 2, 1))
    block, rider = lax.optimization_barrier((block, rider))
    rider = send(rider, hops[1])
    for stride, size in reversed(scatter):
        digit = (me // stride) % size
        piece = block.shape[0]
        whole = jnp.zeros((size * piece,) + block.shape[1:], block.dtype)
        for step in range(size):
            part = send(block, partners(total, stride, size, step)) if step else block
            whole = lax.dynamic_update_slice_in_dim(whole, part, (digit ^ step) * piece, 0)
        block = whole
    return block, rider


def squared_norm(matrix):
    return jnp.sum(matrix * matrix)


def power_start(matrix, rhs, scale_ref, error_ref, value_ref):
    order = matrix.shape[0]
    row, col = square_index(order)
    eye = jnp.where(row == col, 1.0, 0.0).astype(jnp.float32)
    diagonal = matrix * eye
    across = lax.rsqrt(jnp.sum(diagonal, axis=0, keepdims=True))
    scale_ref[...] = lax.rsqrt(jnp.sum(diagonal, axis=1, keepdims=True))
    unit = matrix * across * scale_ref[...]
    error = eye - unit
    square = dot(error, error)
    fourth = dot(square, square)
    start = scale_ref[...] * (eye if rhs is None else rhs)
    value = start + dot(error, start)
    value_ref[...] = value + dot(square, value)
    error_ref[...] = fourth

    @pl.when(jnp.logical_not(squared_norm(fourth) < 0.9))
    def _():
        factor = 1.0 / jnp.max(jnp.sum(jnp.abs(unit), axis=1))
        value_ref[...] = factor * start
        error_ref[...] = eye - factor * unit


def power_step(error_ref, value_ref):
    error = error_ref[...]
    value_ref[...] += dot(error, value_ref[...])
    error_ref[...] = dot(error, error)
    return squared_norm(error)


def solve_kernel(first, grams, alpha, beta, scale, error, value, norm_scale, norm_error, norm_value):
    order = alpha.shape[0]
    norm, square, cross = (grams[at * order : (at + 1) * order] for at in range(3))
    if first:
        curvature = 0.5 * (cross + cross.T)
    else:
        norm, square, curvature = unpack(norm, square)
    power_start(curvature, norm, scale, error, value)
    power_start(norm, None, norm_scale, norm_error, norm_value)

    def both(state):
        return state[0] + 1, jnp.maximum(power_step(error, value), power_step(norm_error, norm_value))

    lax.while_loop(lambda s: (s[0] < MAX_SQUARINGS) & (s[1] > DONE), both, (0, jnp.float32(1.0)))
    step = scale[...] * value[...]
    alpha[...] = step
    change = dot(step.T, dot(square, step) - 2.0 * cross)
    after = norm + 0.5 * (change + change.T)
    beta[...] = norm_scale[...] * dot(norm_value[...], after)


def solve_small(grams, first):
    edits = grams.shape[1]
    square = jax.ShapeDtypeStruct((edits, edits), jnp.float32)
    return pl.pallas_call(
        functools.partial(solve_kernel, first),
        out_shape=[square, square],
        scratch_shapes=[
            pltpu.VMEM((edits, 1), jnp.float32),
            pltpu.VMEM((edits, edits), jnp.float32),
            pltpu.VMEM((edits, edits), jnp.float32),
        ]
        * 2,
        compiler_params=vmem_params(),
        cost_estimate=pl.CostEstimate(flops=0, bytes_accessed=0, transcendentals=0),
    )(grams)


def update_kernel(residual, direction, image, alpha, beta, residual_out, direction_out, lowered_out):
    after = residual[...] - dot_parts(image[...], alpha[...])
    residual_out[...] = after
    following = after + dot(direction[...], beta[...])
    direction_out[...] = following
    lowered_out[...] = following.astype(jnp.bfloat16)


def update(residual, direction, image, alpha, beta):
    rows, edits = residual.shape
    full = jax.ShapeDtypeStruct((rows, edits), jnp.float32)
    return pl.pallas_call(
        update_kernel,
        out_shape=[full, full, jax.ShapeDtypeStruct((rows, edits), jnp.bfloat16)],
        compiler_params=vmem_params(),
        cost_estimate=pl.CostEstimate(
            flops=24 * rows * edits * edits, bytes_accessed=22 * rows * edits, transcendentals=0
        ),
    )(residual, direction, image, alpha, beta)


def advance_kernel(iterate, direction, alpha, out):
    out[...] = iterate[...] + dot(direction[...], alpha[...])


def start_kernel(direction, alpha, out):
    out[...] = dot(direction[...], alpha[...])


def advance(iterate, direction, alpha):
    rows, edits = direction.shape
    return pl.pallas_call(
        start_kernel if iterate is None else advance_kernel,
        out_shape=jax.ShapeDtypeStruct((rows, edits), jnp.float32),
        compiler_params=vmem_params(),
        cost_estimate=pl.CostEstimate(
            flops=12 * rows * edits * edits, bytes_accessed=12 * rows * edits, transcendentals=0
        ),
    )(*([] if iterate is None else [iterate]), direction, alpha)


def body(rows, cols, covariance, right_side):
    total = rows * cols
    order = ring_order(rows)
    me = lax.axis_index("row") * cols + lax.axis_index("col")
    table = index_table(order, cols)
    index = lax.dynamic_index_in_dim(jnp.asarray(table), me, 0, keepdims=False)
    kept = {k: k // cols * cols + quarter_of(k // cols, k % cols, cols) for k in range(total)}
    to_outer = {k: (kept[k] % rows) * cols + kept[k] // rows for k in range(total)}
    swap = {k: k ^ (cols + 1) if (k // cols ^ k) & 1 else k for k in range(total)}
    hops = [list(swap.items()), [(swap[k], to_outer[k]) for k in range(total)]]
    residual = direction = right_side
    lowered = right_side.astype(jnp.bfloat16)
    inner_residual = inner_direction = None
    iterate = alpha = earlier = None
    for iteration in range(ITERS):
        first, last = iteration == 0, iteration == ITERS - 1
        pieces, inner = partial_image(covariance, lowered, order, index, cols, first)
        own, got, (here, before, inner) = exchange_sum(pieces, rows, (residual, earlier, inner))
        norm = local_norm(here)
        if first:
            own, norm = lax.optimization_barrier((own, norm))
            inner_residual = sum(inner[1:], inner[0]).astype(jnp.float32)
            blocks = [inner_residual]
            inner_direction = inner_residual
        else:
            iterate = advance(iterate, before, alpha)
            own, norm, iterate = lax.optimization_barrier((own, norm, iterate))
            blocks = [inner_residual, inner_direction]
        inner_image, grams = local_grams(own, got, norm, blocks)
        grams, image = sum_all(grams, rows, cols, inner_image, hops)
        alpha, beta = solve_small(grams, first)
        earlier = direction
        residual, direction, lowered = update(residual, direction, image, alpha, beta)
        if not last:
            inner_residual, inner_direction, _ = update(
                inner_residual, inner_direction, inner_image, alpha, beta
            )
    return (advance(iterate, earlier, alpha), residual, direction)


def solution(mesh):
    place = P(("col", "row"), None)
    return jax.shard_map(
        functools.partial(body, mesh.shape["row"], mesh.shape["col"]),
        mesh=mesh,
        in_specs=(P("row", "col"), place),
        out_specs=(place, place, place),
        check_vma=False,
    )
```

```python
import functools

import jax
import jax.numpy as jnp
import numpy as np
from jax import lax
from jax.experimental import pallas as pl
from jax.experimental.pallas import tpu as pltpu
from jax.sharding import PartitionSpec as P

ITERS = 3
AXES = ("row", "col")
HIGHEST = lax.Precision.HIGHEST
VMEM_LIMIT = 14 * 1024 * 1024
SLOTS = 3
DONE = 3e-8
MAX_SQUARINGS = 48


def dot(left, right):
    return jnp.dot(left, right, precision=HIGHEST, preferred_element_type=jnp.float32)


def dot_parts(left, right):
    total = None
    for _ in range(3):
        part = right.astype(jnp.bfloat16)
        right = right - part.astype(jnp.float32)
        term = jnp.dot(left, part, preferred_element_type=jnp.float32)
        total = term if total is None else total + term
    return total


def send(block, pairs):
    return lax.ppermute(block, AXES, pairs)


def vmem_params(**extra):
    return pltpu.CompilerParams(vmem_limit_bytes=VMEM_LIMIT, **extra)


def bits_of(size, first_stride):
    assert size & (size - 1) == 0
    return [first_stride << b for b in range(size.bit_length() - 1)]


def ring_order(rows):
    fast = 1 << ((rows.bit_length() - 1) // 2)
    slow = rows // fast
    if fast == 1 or slow == 1:
        return list(range(rows))
    cycle = [s * fast for s in range(slow)]
    for s in reversed(range(slow)):
        lane = range(1, fast) if (slow - 1 - s) % 2 == 0 else reversed(range(1, fast))
        cycle += [s * fast + f for f in lane]
    return cycle


def quarter_of(row, col, cols):
    return col ^ ((row >> 1 & 1) * min(2, cols // 2))


def ring_shifts(rows):
    return [0] + [s for d in range(1, rows // 2) for s in (-d, d)] + [rows // 2]


def index_table(order, cols):
    rows = len(order)
    place = {r: i for i, r in enumerate(order)}

    def line(r, c):
        quarters = [quarter_of(r, c ^ j, cols) for j in range(cols)]
        owners = [order[(place[r] + s) % rows] for s in ring_shifts(rows)]
        return quarters + owners + [owners.index((r * cols + q) % rows) for q in quarters]

    return np.array([line(r, c) for r in range(rows) for c in range(cols)], np.int32)


def pick_kernel(first, count, index, *refs):
    halves, outs = refs[:count], refs[count:]
    half = halves[0].shape[0]
    for j, out in enumerate(outs):
        for at in range(len(halves) // 2):

            @pl.when(index[first + j] == at)
            def _():
                out[0:half, :] = halves[2 * at][...]
                out[half : 2 * half, :] = halves[2 * at + 1][...]


def pick(index, halves, cols, first):
    half, edits = halves[0].shape
    return pl.pallas_call(
        functools.partial(pick_kernel, first, len(halves)),
        in_specs=[pl.BlockSpec(memory_space=pltpu.SMEM)] + [pl.BlockSpec(memory_space=pltpu.VMEM)] * len(halves),
        out_shape=[jax.ShapeDtypeStruct((2 * half, edits), halves[0].dtype)] * cols,
        compiler_params=vmem_params(),
        cost_estimate=pl.CostEstimate(flops=0, bytes_accessed=8 * half * edits * cols, transcendentals=0),
    )(index, *halves)


def spread(picked, rows, cols):
    holders = [r * cols // rows for r in range(rows)]
    kept = jnp.where(lax.axis_index("col") == lax.axis_index("row") * cols // rows, picked[0], jnp.zeros_like(picked[0]))
    return [kept] + [
        send(picked[j], [(r * cols + holders[r], r * cols + (holders[r] ^ j)) for r in range(rows)])
        for j in range(cols - 1, 0, -1)
    ]


def chunk_kernel(blocks, halves, has_base, cols, first_owner, begin, count, index, cov, *refs):
    parts = refs[: blocks * halves]
    base = refs[blocks * halves] if has_base else None
    outs, (tiles, arrived, joined) = refs[blocks * halves + has_base : -3], refs[-3:]
    piece = parts[0].shape[0]
    depth = piece * halves
    height = tiles.shape[1]

    def fetch(step, t):
        slot = lax.rem(step, SLOTS)
        row = pl.multiple_of(index[begin + step] * height, 16)
        col = pl.multiple_of(index[cols + first_owner + t] * depth, 128)
        return pltpu.make_async_copy(
            cov.at[pl.ds(row, height), pl.ds(col, depth)],
            tiles.at[slot, :, pl.ds(t * depth, depth)],
            arrived.at[slot, t],
        )

    for step in range(min(SLOTS - 1, count)):
        for t in range(blocks):
            fetch(jnp.int32(step), t).start()
    for at, part in enumerate(parts):
        joined[at * piece : (at + 1) * piece, :] = part[...]

    def one(step, carry):
        @pl.when(step + SLOTS - 1 < count)
        def _():
            for t in range(blocks):
                fetch(step + SLOTS - 1, t).start()

        for t in range(blocks):
            fetch(step, t).wait()
        slot = lax.rem(step, SLOTS)
        term = jnp.dot(tiles[slot], joined[...], preferred_element_type=jnp.float32)
        if has_base:
            term = term + base[pl.ds(pl.multiple_of((begin + step) * height, 16), height), :]
        if len(outs) == 1:
            outs[0][pl.ds(pl.multiple_of(step * height, 16), height), :] = term
        for at, out in enumerate(outs if len(outs) > 1 else ()):

            @pl.when(step == at)
            def _():
                out[...] = term

        return carry

    lax.fori_loop(0, count, one, 0)


def add_chunks(covariance, index, cols, first_owner, parts, halves, base, begin, count):
    outs = 1 if count == cols else count
    blocks = len(parts) // halves
    piece, edits = parts[0].shape
    depth = piece * halves
    height = covariance.shape[0] // cols
    has_base = base is not None
    operands = [index, covariance] + list(parts) + ([base] if has_base else [])
    in_vmem = pl.BlockSpec(memory_space=pltpu.VMEM)
    return pl.pallas_call(
        functools.partial(chunk_kernel, blocks, halves, has_base, cols, first_owner, begin, count),
        in_specs=[pl.BlockSpec(memory_space=pltpu.SMEM), pl.BlockSpec(memory_space=pl.ANY)]
        + [in_vmem] * (len(operands) - 2),
        out_specs=[in_vmem] * outs,
        out_shape=[jax.ShapeDtypeStruct((count // outs * height, edits), jnp.float32)] * outs,
        scratch_shapes=[
            pltpu.VMEM((SLOTS, height, blocks * depth), jnp.bfloat16),
            pltpu.SemaphoreType.DMA((SLOTS, blocks)),
            pltpu.VMEM((blocks * depth, edits), jnp.bfloat16),
        ],
        input_output_aliases={len(operands) - 1: 0} if has_base and count == cols else {},
        compiler_params=vmem_params(),
        cost_estimate=pl.CostEstimate(
            flops=2 * count * height * depth * blocks * edits,
            bytes_accessed=2 * count * height * depth * blocks,
            transcendentals=0,
        ),
    )(*operands)


def partial_image(covariance, lowered, order, index, cols, first):
    rows = len(order)
    depth = lowered.shape[0]
    quarter = covariance.shape[0] // cols
    if depth % 128 or depth % 32 or quarter % 16 or rows % 2:
        whole = lax.all_gather(lowered, "row", axis=0, tiled=True)
        product = jnp.dot(covariance, whole, preferred_element_type=jnp.float32)
        swapped = product.reshape(cols, quarter, -1)[index[:cols]]
        inner = None
        if first:
            blocks = [
                lax.dynamic_slice_in_dim(whole, (lax.axis_index("row") * cols + index[j]) % rows * depth, depth, 0)
                for j in range(cols)
            ]
            inner = spread(blocks, rows, cols)
        return [swapped[j] for j in range(cols)], inner
    following = {order[i]: order[(i + 1) % rows] for i in range(rows)}
    forward = [(r * cols + c, following[r] * cols + c) for r in range(rows) for c in range(cols)]
    backward = [(b, a) for a, b in forward]
    half = depth // 2
    behind = ahead = [lowered[:half], lowered[half:]]
    held, owner, total = behind, 0, None
    seen = list(held)
    for step in range(1, rows // 2 + 1):
        if step < rows // 2:
            pairs = [(send(low, forward), send(high, backward)) for low, high in zip(behind, ahead)]
            behind, ahead = zip(*pairs)
            arrived = list(behind) + list(ahead)
        else:
            arrived = [send(behind[0], forward), send(ahead[1], backward)]
        (total,) = add_chunks(covariance, index, cols, owner, held, 2, total, 0, cols)
        owner += len(held) // 2
        if step < rows // 2:
            total, low, high = lax.optimization_barrier((total, behind[0], ahead[0]))
            behind, ahead = [low, behind[1]], [high, ahead[1]]
            arrived = behind + ahead
        held = arrived
        seen += arrived
    inner = None
    if first:
        picked = pick(index, seen, cols, cols + rows)
        total, picked = lax.optimization_barrier((total, picked))
        inner = spread(picked, rows, cols)
    upper = add_chunks(covariance, index, cols, owner, held, 2, total, cols // 2, cols // 2)
    lower = add_chunks(covariance, index, cols, owner, held, 2, total, 0, cols // 2)
    return list(lower) + list(upper), inner


def exchange_sum(pieces, rows, others):
    cols = len(pieces)
    far = cols // 2

    def fold(held):
        for bit in bits_of(far, 1):
            pairs = [(i, i ^ bit) for i in range(rows * cols)]
            got = {}
            for j in sorted((j for j in held if j & bit), reverse=True):
                block = held[j].astype(jnp.bfloat16) if bit > 1 else held[j]
                got[j ^ bit] = send(block, pairs)
            held = {j: held[j] + got[j].astype(jnp.float32) for j in got}
        return held

    leaving = fold({j: pieces[j] for j in range(far, cols)})[far].astype(jnp.bfloat16)
    leaving, others = lax.optimization_barrier((leaving, others))
    got = send(leaving, [(i, i ^ far) for i in range(rows * cols)])
    return fold(dict(enumerate(pieces[:far])))[0], got, others


def norm_kernel(residual, out):
    value = residual[...]
    out[...] = dot(value.T, value)


def local_norm(residual):
    rows, edits = residual.shape
    return pl.pallas_call(
        norm_kernel,
        out_shape=jax.ShapeDtypeStruct((edits, edits), jnp.float32),
        compiler_params=vmem_params(),
        cost_estimate=pl.CostEstimate(
            flops=12 * rows * edits * edits, bytes_accessed=4 * rows * edits, transcendentals=0
        ),
    )(residual)


def square_index(order):
    shape = (order, order)
    return lax.broadcasted_iota(jnp.int32, shape, 0), lax.broadcasted_iota(jnp.int32, shape, 1)


def pack(norm, square, curvature):
    row, col = square_index(norm.shape[0])
    diagonal = jnp.sum(jnp.where(row == col, square, 0.0), axis=1, keepdims=True)
    below = jnp.where(col == 0, diagonal, diagonal[0:1, 0:1])
    return jnp.where(col >= row, norm, below), jnp.where(col >= row, curvature, square)


def unpack(with_norm, with_curvature):
    row, col = square_index(with_norm.shape[0])

    def mirror(half, diagonal):
        return jnp.where(row == col, diagonal, half + half.T)

    norm = mirror(jnp.where(col > row, with_norm, 0.0), with_norm)
    curvature = mirror(jnp.where(col > row, with_curvature, 0.0), with_curvature)
    diagonal = jnp.where(row == 0, with_norm[2:3, 1:2], with_norm[:, 0:1])
    return norm, mirror(jnp.where(col < row, with_curvature, 0.0), diagonal), curvature


def gram_kernel(own, got, norm, *refs):
    image, grams = refs[-2:]
    value = (own[...] + got[...].astype(jnp.float32)).astype(jnp.bfloat16)
    image[...] = value
    order = value.shape[1]
    flipped = value.T
    square = jnp.dot(flipped, value, preferred_element_type=jnp.float32)
    cross = dot_parts(flipped, refs[0][...])
    if len(refs) == 3:
        grams[0:order], grams[order : 2 * order] = norm[...], square
    else:
        curvature = dot_parts(flipped, refs[1][...])
        curvature = 0.5 * (curvature + curvature.T)
        grams[0:order], grams[order : 2 * order] = pack(norm[...], square, curvature)
    grams[2 * order :] = cross


def local_grams(own, got, norm, blocks):
    rows, edits = own.shape
    return pl.pallas_call(
        gram_kernel,
        out_shape=[
            jax.ShapeDtypeStruct((rows, edits), jnp.bfloat16),
            jax.ShapeDtypeStruct((3 * edits, edits), jnp.float32),
        ],
        compiler_params=vmem_params(),
        cost_estimate=pl.CostEstimate(
            flops=14 * rows * edits * edits, bytes_accessed=16 * rows * edits, transcendentals=0
        ),
    )(own, got, norm, *blocks)


def partners(total, stride, size, step):
    return [(i, i + (((i // stride) % size ^ step) - (i // stride) % size) * stride) for i in range(total)]


def sum_all(block, rows, cols, rider, hops):
    total = rows * cols
    me = lax.axis_index("row") * cols + lax.axis_index("col")
    plane = cols // 2 * min(2, rows)
    scatter = [(1, 2), (2, plane)]
    exchange = [(stride, 2) for stride in bits_of(total // (2 * plane), 2 * plane)]
    for stride, size in scatter:
        digit = (me // stride) % size
        piece = block.shape[0] // size
        got = [
            send(lax.dynamic_slice_in_dim(block, (digit ^ step) * piece, piece, 0), partners(total, stride, size, step))
            for step in range(1, size)
        ]
        block = lax.dynamic_slice_in_dim(block, digit * piece, piece, 0)
        for term in got:
            block = block + term
    block, rider = lax.optimization_barrier((block, rider))
    rider = send(rider, hops[0])
    for stride, _ in exchange:
        block = block + send(block, partners(total, stride, 2, 1))
    block, rider = lax.optimization_barrier((block, rider))
    rider = send(rider, hops[1])
    for stride, size in reversed(scatter):
        digit = (me // stride) % size
        piece = block.shape[0]
        whole = jnp.zeros((size * piece,) + block.shape[1:], block.dtype)
        for step in range(size):
            part = send(block, partners(total, stride, size, step)) if step else block
            whole = lax.dynamic_update_slice_in_dim(whole, part, (digit ^ step) * piece, 0)
        block = whole
    return block, rider


def squared_norm(matrix):
    return jnp.sum(matrix * matrix)


def power_start(matrix, rhs, scale_ref, error_ref, value_ref):
    order = matrix.shape[0]
    row, col = square_index(order)
    eye = jnp.where(row == col, 1.0, 0.0).astype(jnp.float32)
    diagonal = matrix * eye
    across = lax.rsqrt(jnp.sum(diagonal, axis=0, keepdims=True))
    scale_ref[...] = lax.rsqrt(jnp.sum(diagonal, axis=1, keepdims=True))
    unit = matrix * across * scale_ref[...]
    error = eye - unit
    square = dot(error, error)
    fourth = dot(square, square)
    start = scale_ref[...] * (eye if rhs is None else rhs)
    value = start + dot(error, start)
    value_ref[...] = value + dot(square, value)
    error_ref[...] = fourth

    @pl.when(jnp.logical_not(squared_norm(fourth) < 0.9))
    def _():
        factor = 1.0 / jnp.max(jnp.sum(jnp.abs(unit), axis=1))
        value_ref[...] = factor * start
        error_ref[...] = eye - factor * unit


def power_step(error_ref, value_ref):
    error = error_ref[...]
    value_ref[...] += dot(error, value_ref[...])
    error_ref[...] = dot(error, error)
    return squared_norm(error)


def solve_kernel(first, grams, alpha, beta, scale, error, value, norm_scale, norm_error, norm_value):
    order = alpha.shape[0]
    norm, square, cross = (grams[at * order : (at + 1) * order] for at in range(3))
    if first:
        curvature = 0.5 * (cross + cross.T)
    else:
        norm, square, curvature = unpack(norm, square)
    power_start(curvature, norm, scale, error, value)
    power_start(norm, None, norm_scale, norm_error, norm_value)

    def both(state):
        return state[0] + 1, jnp.maximum(power_step(error, value), power_step(norm_error, norm_value))

    lax.while_loop(lambda s: (s[0] < MAX_SQUARINGS) & (s[1] > DONE), both, (0, jnp.float32(1.0)))
    step = scale[...] * value[...]
    alpha[...] = step
    change = dot(step.T, dot(square, step) - 2.0 * cross)
    after = norm + 0.5 * (change + change.T)
    beta[...] = norm_scale[...] * dot(norm_value[...], after)


def solve_small(grams, first):
    edits = grams.shape[1]
    square = jax.ShapeDtypeStruct((edits, edits), jnp.float32)
    return pl.pallas_call(
        functools.partial(solve_kernel, first),
        out_shape=[square, square],
        scratch_shapes=[
            pltpu.VMEM((edits, 1), jnp.float32),
            pltpu.VMEM((edits, edits), jnp.float32),
            pltpu.VMEM((edits, edits), jnp.float32),
        ]
        * 2,
        compiler_params=vmem_params(),
        cost_estimate=pl.CostEstimate(flops=0, bytes_accessed=0, transcendentals=0),
    )(grams)


def update_kernel(residual, direction, image, alpha, beta, residual_out, direction_out, lowered_out):
    after = residual[...] - dot_parts(image[...], alpha[...])
    residual_out[...] = after
    following = after + dot(direction[...], beta[...])
    direction_out[...] = following
    lowered_out[...] = following.astype(jnp.bfloat16)


def finish_kernel(iterate, residual, direction, image, alpha, beta, iterate_out, residual_out, direction_out):
    iterate_out[...] = iterate[...] + dot(direction[...], alpha[...])
    after = residual[...] - dot_parts(image[...], alpha[...])
    residual_out[...] = after
    direction_out[...] = after + dot(direction[...], beta[...])


def finish(iterate, residual, direction, image, alpha, beta):
    rows, edits = residual.shape
    return pl.pallas_call(
        finish_kernel,
        out_shape=[jax.ShapeDtypeStruct((rows, edits), jnp.float32)] * 3,
        compiler_params=vmem_params(),
        cost_estimate=pl.CostEstimate(
            flops=30 * rows * edits * edits, bytes_accessed=30 * rows * edits, transcendentals=0
        ),
    )(iterate, residual, direction, image, alpha, beta)


def update(residual, direction, image, alpha, beta):
    rows, edits = residual.shape
    full = jax.ShapeDtypeStruct((rows, edits), jnp.float32)
    return pl.pallas_call(
        update_kernel,
        out_shape=[full, full, jax.ShapeDtypeStruct((rows, edits), jnp.bfloat16)],
        compiler_params=vmem_params(),
        cost_estimate=pl.CostEstimate(
            flops=24 * rows * edits * edits, bytes_accessed=22 * rows * edits, transcendentals=0
        ),
    )(residual, direction, image, alpha, beta)


def advance_kernel(iterate, direction, alpha, out):
    out[...] = iterate[...] + dot(direction[...], alpha[...])


def start_kernel(direction, alpha, out):
    out[...] = dot(direction[...], alpha[...])


def advance(iterate, direction, alpha):
    rows, edits = direction.shape
    return pl.pallas_call(
        start_kernel if iterate is None else advance_kernel,
        out_shape=jax.ShapeDtypeStruct((rows, edits), jnp.float32),
        compiler_params=vmem_params(),
        cost_estimate=pl.CostEstimate(
            flops=12 * rows * edits * edits, bytes_accessed=12 * rows * edits, transcendentals=0
        ),
    )(*([] if iterate is None else [iterate]), direction, alpha)


def body(rows, cols, covariance, right_side):
    total = rows * cols
    order = ring_order(rows)
    me = lax.axis_index("row") * cols + lax.axis_index("col")
    table = index_table(order, cols)
    index = lax.dynamic_index_in_dim(jnp.asarray(table), me, 0, keepdims=False)
    kept = {k: k // cols * cols + quarter_of(k // cols, k % cols, cols) for k in range(total)}
    to_outer = {k: (kept[k] % rows) * cols + kept[k] // rows for k in range(total)}
    swap = {k: k ^ (cols + 1) if (k // cols ^ k) & 1 else k for k in range(total)}
    hops = [list(swap.items()), [(swap[k], to_outer[k]) for k in range(total)]]
    residual = direction = right_side
    lowered = right_side.astype(jnp.bfloat16)
    inner_residual = inner_direction = None
    iterate = alpha = earlier = None
    for iteration in range(ITERS):
        first, last = iteration == 0, iteration == ITERS - 1
        pieces, inner = partial_image(covariance, lowered, order, index, cols, first)
        own, got, (here, before) = exchange_sum(pieces, rows, (residual, earlier))
        norm = local_norm(here)
        if first:
            own, norm = lax.optimization_barrier((own, norm))
            inner_residual = sum(inner[1:], inner[0]).astype(jnp.float32)
            blocks = [inner_residual]
            inner_direction = inner_residual
        else:
            iterate = advance(iterate, before, alpha)
            own, norm, iterate = lax.optimization_barrier((own, norm, iterate))
            blocks = [inner_residual, inner_direction]
        inner_image, grams = local_grams(own, got, norm, blocks)
        grams, image = sum_all(grams, rows, cols, inner_image, hops)
        alpha, beta = solve_small(grams, first)
        if last:
            break
        earlier = direction
        residual, direction, lowered = update(residual, direction, image, alpha, beta)
        inner_residual, inner_direction, _ = update(inner_residual, inner_direction, inner_image, alpha, beta)
    return tuple(finish(iterate, residual, direction, image, alpha, beta))


def solution(mesh):
    place = P(("col", "row"), None)
    return jax.shard_map(
        functools.partial(body, mesh.shape["row"], mesh.shape["col"]),
        mesh=mesh,
        in_specs=(P("row", "col"), place),
        out_specs=(place, place, place),
        check_vma=False,
    )
```

```python
import functools

import jax
import jax.numpy as jnp
import numpy as np
from jax import lax
from jax.experimental import pallas as pl
from jax.experimental.pallas import tpu as pltpu
from jax.sharding import PartitionSpec as P

ITERS = 3
AXES = ("row", "col")
HIGHEST = lax.Precision.HIGHEST
VMEM_LIMIT = 14 * 1024 * 1024
SLOTS = 3
DONE = 3e-8
MAX_SQUARINGS = 48


def dot(left, right):
    return jnp.dot(left, right, precision=HIGHEST, preferred_element_type=jnp.float32)


def dot_parts(left, right):
    total = None
    for _ in range(3):
        part = right.astype(jnp.bfloat16)
        right = right - part.astype(jnp.float32)
        term = jnp.dot(left, part, preferred_element_type=jnp.float32)
        total = term if total is None else total + term
    return total


def send(block, pairs):
    return lax.ppermute(block, AXES, pairs)


def vmem_params(**extra):
    return pltpu.CompilerParams(vmem_limit_bytes=VMEM_LIMIT, **extra)


def bits_of(size, first_stride):
    assert size & (size - 1) == 0
    return [first_stride << b for b in range(size.bit_length() - 1)]


def ring_order(rows):
    fast = 1 << ((rows.bit_length() - 1) // 2)
    slow = rows // fast
    if fast == 1 or slow == 1:
        return list(range(rows))
    cycle = [s * fast for s in range(slow)]
    for s in reversed(range(slow)):
        lane = range(1, fast) if (slow - 1 - s) % 2 == 0 else reversed(range(1, fast))
        cycle += [s * fast + f for f in lane]
    return cycle


def quarter_of(row, col, cols):
    return col ^ ((row >> 1 & 1) * min(2, cols // 2))


def ring_shifts(rows):
    return [0] + [s for d in range(1, rows // 2) for s in (-d, d)] + [rows // 2]


def index_table(order, cols):
    rows = len(order)
    place = {r: i for i, r in enumerate(order)}

    def line(r, c):
        quarters = [quarter_of(r, c ^ j, cols) for j in range(cols)]
        owners = [order[(place[r] + s) % rows] for s in ring_shifts(rows)]
        return quarters + owners + [owners.index((r * cols + q) % rows) for q in quarters]

    return np.array([line(r, c) for r in range(rows) for c in range(cols)], np.int32)


def pick_kernel(first, count, index, *refs):
    halves, outs = refs[:count], refs[count:]
    half = halves[0].shape[0]
    for j, out in enumerate(outs):
        for at in range(len(halves) // 2):

            @pl.when(index[first + j] == at)
            def _():
                out[0:half, :] = halves[2 * at][...]
                out[half : 2 * half, :] = halves[2 * at + 1][...]


def pick(index, halves, cols, first):
    half, edits = halves[0].shape
    return pl.pallas_call(
        functools.partial(pick_kernel, first, len(halves)),
        in_specs=[pl.BlockSpec(memory_space=pltpu.SMEM)] + [pl.BlockSpec(memory_space=pltpu.VMEM)] * len(halves),
        out_shape=[jax.ShapeDtypeStruct((2 * half, edits), halves[0].dtype)] * cols,
        compiler_params=vmem_params(),
        cost_estimate=pl.CostEstimate(flops=0, bytes_accessed=8 * half * edits * cols, transcendentals=0),
    )(index, *halves)


def spread(picked, rows, cols):
    holders = [r * cols // rows for r in range(rows)]
    kept = jnp.where(lax.axis_index("col") == lax.axis_index("row") * cols // rows, picked[0], jnp.zeros_like(picked[0]))
    return [kept] + [
        send(picked[j], [(r * cols + holders[r], r * cols + (holders[r] ^ j)) for r in range(rows)])
        for j in range(cols - 1, 0, -1)
    ]


def chunk_kernel(blocks, halves, has_base, cols, first_owner, begin, count, index, cov, *refs):
    parts = refs[: blocks * halves]
    base = refs[blocks * halves] if has_base else None
    out, tiles, arrived, joined = refs[-4:]
    piece = parts[0].shape[0]
    depth = piece * halves
    height = tiles.shape[1]

    def fetch(step, t):
        slot = lax.rem(step, SLOTS)
        row = pl.multiple_of(index[begin + step] * height, 16)
        col = pl.multiple_of(index[cols + first_owner + t] * depth, 128)
        return pltpu.make_async_copy(
            cov.at[pl.ds(row, height), pl.ds(col, depth)],
            tiles.at[slot, :, pl.ds(t * depth, depth)],
            arrived.at[slot, t],
        )

    for step in range(min(SLOTS - 1, count)):
        for t in range(blocks):
            fetch(jnp.int32(step), t).start()
    for at, part in enumerate(parts):
        joined[at * piece : (at + 1) * piece, :] = part[...]

    def one(step, carry):
        @pl.when(step + SLOTS - 1 < count)
        def _():
            for t in range(blocks):
                fetch(step + SLOTS - 1, t).start()

        for t in range(blocks):
            fetch(step, t).wait()
        slot = lax.rem(step, SLOTS)
        term = jnp.dot(tiles[slot], joined[...], preferred_element_type=jnp.float32)
        if has_base:
            term = term + base[pl.ds(pl.multiple_of((begin + step) * height, 16), height), :]
        out[pl.ds(pl.multiple_of(step * height, 16), height), :] = term
        return carry

    lax.fori_loop(0, count, one, 0)


def add_chunks(covariance, index, cols, first_owner, parts, halves, base, begin, count):
    blocks = len(parts) // halves
    piece, edits = parts[0].shape
    depth = piece * halves
    height = covariance.shape[0] // cols
    has_base = base is not None
    operands = [index, covariance] + list(parts) + ([base] if has_base else [])
    in_vmem = pl.BlockSpec(memory_space=pltpu.VMEM)
    return pl.pallas_call(
        functools.partial(chunk_kernel, blocks, halves, has_base, cols, first_owner, begin, count),
        in_specs=[pl.BlockSpec(memory_space=pltpu.SMEM), pl.BlockSpec(memory_space=pl.ANY)]
        + [in_vmem] * (len(operands) - 2),
        out_specs=in_vmem,
        out_shape=jax.ShapeDtypeStruct((count * height, edits), jnp.float32),
        scratch_shapes=[
            pltpu.VMEM((SLOTS, height, blocks * depth), jnp.bfloat16),
            pltpu.SemaphoreType.DMA((SLOTS, blocks)),
            pltpu.VMEM((blocks * depth, edits), jnp.bfloat16),
        ],
        input_output_aliases={len(operands) - 1: 0} if has_base and count == cols else {},
        compiler_params=vmem_params(),
        cost_estimate=pl.CostEstimate(
            flops=2 * count * height * depth * blocks * edits,
            bytes_accessed=2 * count * height * depth * blocks,
            transcendentals=0,
        ),
    )(*operands)


def partial_image(covariance, lowered, order, index, cols, first):
    rows = len(order)
    depth = lowered.shape[0]
    quarter = covariance.shape[0] // cols
    if depth % 128 or depth % 32 or quarter % 16 or rows % 2:
        whole = lax.all_gather(lowered, "row", axis=0, tiled=True)
        product = jnp.dot(covariance, whole, preferred_element_type=jnp.float32)
        swapped = product.reshape(cols, quarter, -1)[index[:cols]]
        inner = None
        if first:
            blocks = [
                lax.dynamic_slice_in_dim(whole, (lax.axis_index("row") * cols + index[j]) % rows * depth, depth, 0)
                for j in range(cols)
            ]
            inner = spread(blocks, rows, cols)
        return [swapped[j] for j in range(cols)], inner
    following = {order[i]: order[(i + 1) % rows] for i in range(rows)}
    forward = [(r * cols + c, following[r] * cols + c) for r in range(rows) for c in range(cols)]
    backward = [(b, a) for a, b in forward]
    half = depth // 2
    behind = ahead = [lowered[:half], lowered[half:]]
    held, owner, total = behind, 0, None
    seen = list(held)
    for step in range(1, rows // 2 + 1):
        if step < rows // 2:
            pairs = [(send(low, forward), send(high, backward)) for low, high in zip(behind, ahead)]
            behind, ahead = zip(*pairs)
            arrived = list(behind) + list(ahead)
        else:
            arrived = [send(behind[0], forward), send(ahead[1], backward)]
        total = add_chunks(covariance, index, cols, owner, held, 2, total, 0, cols)
        owner += len(held) // 2
        if step < rows // 2:
            total, low, high = lax.optimization_barrier((total, behind[0], ahead[0]))
            behind, ahead = [low, behind[1]], [high, ahead[1]]
            arrived = behind + ahead
        held = arrived
        seen += arrived
    inner = None
    if first:
        picked = pick(index, seen, cols, cols + rows)
        total, picked = lax.optimization_barrier((total, picked))
        inner = spread(picked, rows, cols)
    upper = add_chunks(covariance, index, cols, owner, held, 2, total, cols // 2, cols // 2)
    lower = add_chunks(covariance, index, cols, owner, held, 2, total, 0, cols // 2)
    return [part[j * quarter : (j + 1) * quarter] for part in (lower, upper) for j in range(cols // 2)], inner


def exchange_sum(pieces, rows, others):
    cols = len(pieces)
    far = cols // 2

    def fold(held):
        for bit in bits_of(far, 1):
            pairs = [(i, i ^ bit) for i in range(rows * cols)]
            got = {}
            for j in sorted((j for j in held if j & bit), reverse=True):
                block = held[j].astype(jnp.bfloat16) if bit > 1 else held[j]
                got[j ^ bit] = send(block, pairs)
            held = {j: held[j] + got[j].astype(jnp.float32) for j in got}
        return held

    leaving = fold({j: pieces[j] for j in range(far, cols)})[far].astype(jnp.bfloat16)
    leaving, others = lax.optimization_barrier((leaving, others))
    got = send(leaving, [(i, i ^ far) for i in range(rows * cols)])
    return fold(dict(enumerate(pieces[:far])))[0], got, others


def norm_kernel(residual, out):
    value = residual[...]
    out[...] = dot(value.T, value)


def local_norm(residual):
    rows, edits = residual.shape
    return pl.pallas_call(
        norm_kernel,
        out_shape=jax.ShapeDtypeStruct((edits, edits), jnp.float32),
        compiler_params=vmem_params(),
        cost_estimate=pl.CostEstimate(
            flops=12 * rows * edits * edits, bytes_accessed=4 * rows * edits, transcendentals=0
        ),
    )(residual)


def square_index(order):
    shape = (order, order)
    return lax.broadcasted_iota(jnp.int32, shape, 0), lax.broadcasted_iota(jnp.int32, shape, 1)


def pack(norm, square, curvature):
    row, col = square_index(norm.shape[0])
    diagonal = jnp.sum(jnp.where(row == col, square, 0.0), axis=1, keepdims=True)
    below = jnp.where(col == 0, diagonal, diagonal[0:1, 0:1])
    return jnp.where(col >= row, norm, below), jnp.where(col >= row, curvature, square)


def unpack(with_norm, with_curvature):
    row, col = square_index(with_norm.shape[0])

    def mirror(half, diagonal):
        return jnp.where(row == col, diagonal, half + half.T)

    norm = mirror(jnp.where(col > row, with_norm, 0.0), with_norm)
    curvature = mirror(jnp.where(col > row, with_curvature, 0.0), with_curvature)
    diagonal = jnp.where(row == 0, with_norm[2:3, 1:2], with_norm[:, 0:1])
    return norm, mirror(jnp.where(col < row, with_curvature, 0.0), diagonal), curvature


def gram_kernel(own, got, norm, *refs):
    image, grams = refs[-2:]
    value = (own[...] + got[...].astype(jnp.float32)).astype(jnp.bfloat16)
    image[...] = value
    order = value.shape[1]
    flipped = value.T
    square = jnp.dot(flipped, value, preferred_element_type=jnp.float32)
    cross = dot_parts(flipped, refs[0][...])
    if len(refs) == 3:
        grams[0:order], grams[order : 2 * order] = norm[...], square
    else:
        curvature = dot_parts(flipped, refs[1][...])
        curvature = 0.5 * (curvature + curvature.T)
        grams[0:order], grams[order : 2 * order] = pack(norm[...], square, curvature)
    grams[2 * order :] = cross


def local_grams(own, got, norm, blocks):
    rows, edits = own.shape
    return pl.pallas_call(
        gram_kernel,
        out_shape=[
            jax.ShapeDtypeStruct((rows, edits), jnp.bfloat16),
            jax.ShapeDtypeStruct((3 * edits, edits), jnp.float32),
        ],
        compiler_params=vmem_params(),
        cost_estimate=pl.CostEstimate(
            flops=14 * rows * edits * edits, bytes_accessed=16 * rows * edits, transcendentals=0
        ),
    )(own, got, norm, *blocks)


def partners(total, stride, size, step):
    return [(i, i + (((i // stride) % size ^ step) - (i // stride) % size) * stride) for i in range(total)]


def sum_all(block, rows, cols, rider, hops):
    total = rows * cols
    me = lax.axis_index("row") * cols + lax.axis_index("col")
    plane = cols // 2 * min(2, rows)
    scatter = [(1, 2), (2, plane)]
    exchange = [(stride, 2) for stride in bits_of(total // (2 * plane), 2 * plane)]
    for stride, size in scatter:
        digit = (me // stride) % size
        piece = block.shape[0] // size
        got = [
            send(lax.dynamic_slice_in_dim(block, (digit ^ step) * piece, piece, 0), partners(total, stride, size, step))
            for step in range(1, size)
        ]
        block = lax.dynamic_slice_in_dim(block, digit * piece, piece, 0)
        for term in got:
            block = block + term
    block, rider = lax.optimization_barrier((block, rider))
    rider = send(rider, hops[0])
    for stride, _ in exchange:
        block = block + send(block, partners(total, stride, 2, 1))
    block, rider = lax.optimization_barrier((block, rider))
    rider = send(rider, hops[1])
    for stride, size in reversed(scatter):
        digit = (me // stride) % size
        piece = block.shape[0]
        whole = jnp.zeros((size * piece,) + block.shape[1:], block.dtype)
        for step in range(size):
            part = send(block, partners(total, stride, size, step)) if step else block
            whole = lax.dynamic_update_slice_in_dim(whole, part, (digit ^ step) * piece, 0)
        block = whole
    return block, rider


def squared_norm(matrix):
    return jnp.sum(matrix * matrix)


def power_start(matrix, rhs, scale_ref, error_ref, value_ref):
    order = matrix.shape[0]
    row, col = square_index(order)
    eye = jnp.where(row == col, 1.0, 0.0).astype(jnp.float32)
    diagonal = matrix * eye
    across = lax.rsqrt(jnp.sum(diagonal, axis=0, keepdims=True))
    scale_ref[...] = lax.rsqrt(jnp.sum(diagonal, axis=1, keepdims=True))
    unit = matrix * across * scale_ref[...]
    error = eye - unit
    square = dot(error, error)
    fourth = dot(square, square)
    start = scale_ref[...] * (eye if rhs is None else rhs)
    value = start + (error * across if rhs is None else dot(error, start))
    value_ref[...] = value + dot(square, value)
    error_ref[...] = fourth

    @pl.when(jnp.logical_not(squared_norm(fourth) < 0.9))
    def _():
        factor = 1.0 / jnp.max(jnp.sum(jnp.abs(unit), axis=1))
        value_ref[...] = factor * start
        error_ref[...] = eye - factor * unit


def power_step(error_ref, value_ref):
    error = error_ref[...]
    value_ref[...] += dot(error, value_ref[...])
    error_ref[...] = dot(error, error)
    return squared_norm(error)


def solve_kernel(first, grams, alpha, beta, scale, error, value, norm_scale, norm_error, norm_value):
    order = alpha.shape[0]
    norm, square, cross = (grams[at * order : (at + 1) * order] for at in range(3))
    if first:
        curvature = 0.5 * (cross + cross.T)
    else:
        norm, square, curvature = unpack(norm, square)
    power_start(curvature, norm, scale, error, value)
    power_start(norm, None, norm_scale, norm_error, norm_value)

    def both(state):
        return state[0] + 1, jnp.maximum(power_step(error, value), power_step(norm_error, norm_value))

    lax.while_loop(lambda s: (s[0] < MAX_SQUARINGS) & (s[1] > DONE), both, (0, jnp.float32(1.0)))
    step = scale[...] * value[...]
    alpha[...] = step
    change = dot(step.T, dot(square, step) - 2.0 * cross)
    after = norm + 0.5 * (change + change.T)
    beta[...] = norm_scale[...] * dot(norm_value[...], after)


def solve_small(grams, first):
    edits = grams.shape[1]
    square = jax.ShapeDtypeStruct((edits, edits), jnp.float32)
    return pl.pallas_call(
        functools.partial(solve_kernel, first),
        out_shape=[square, square],
        scratch_shapes=[
            pltpu.VMEM((edits, 1), jnp.float32),
            pltpu.VMEM((edits, edits), jnp.float32),
            pltpu.VMEM((edits, edits), jnp.float32),
        ]
        * 2,
        compiler_params=vmem_params(),
        cost_estimate=pl.CostEstimate(flops=0, bytes_accessed=0, transcendentals=0),
    )(grams)


def update_kernel(residual, direction, image, alpha, beta, residual_out, direction_out, lowered_out):
    after = residual[...] - dot_parts(image[...], alpha[...])
    residual_out[...] = after
    following = after + dot(direction[...], beta[...])
    direction_out[...] = following
    lowered_out[...] = following.astype(jnp.bfloat16)


def update(residual, direction, image, alpha, beta):
    rows, edits = residual.shape
    full = jax.ShapeDtypeStruct((rows, edits), jnp.float32)
    return pl.pallas_call(
        update_kernel,
        out_shape=[full, full, jax.ShapeDtypeStruct((rows, edits), jnp.bfloat16)],
        compiler_params=vmem_params(),
        cost_estimate=pl.CostEstimate(
            flops=24 * rows * edits * edits, bytes_accessed=22 * rows * edits, transcendentals=0
        ),
    )(residual, direction, image, alpha, beta)


def advance_kernel(iterate, direction, alpha, out):
    out[...] = iterate[...] + dot(direction[...], alpha[...])


def start_kernel(direction, alpha, out):
    out[...] = dot(direction[...], alpha[...])


def advance(iterate, direction, alpha):
    rows, edits = direction.shape
    return pl.pallas_call(
        start_kernel if iterate is None else advance_kernel,
        out_shape=jax.ShapeDtypeStruct((rows, edits), jnp.float32),
        compiler_params=vmem_params(),
        cost_estimate=pl.CostEstimate(
            flops=12 * rows * edits * edits, bytes_accessed=12 * rows * edits, transcendentals=0
        ),
    )(*([] if iterate is None else [iterate]), direction, alpha)


def body(rows, cols, covariance, right_side):
    total = rows * cols
    order = ring_order(rows)
    me = lax.axis_index("row") * cols + lax.axis_index("col")
    table = index_table(order, cols)
    index = lax.dynamic_index_in_dim(jnp.asarray(table), me, 0, keepdims=False)
    kept = {k: k // cols * cols + quarter_of(k // cols, k % cols, cols) for k in range(total)}
    to_outer = {k: (kept[k] % rows) * cols + kept[k] // rows for k in range(total)}
    swap = {k: k ^ (cols + 1) if (k // cols ^ k) & 1 else k for k in range(total)}
    hops = [list(swap.items()), [(swap[k], to_outer[k]) for k in range(total)]]
    residual = direction = right_side
    lowered = right_side.astype(jnp.bfloat16)
    inner_residual = inner_direction = None
    iterate = alpha = earlier = None
    for iteration in range(ITERS):
        first, last = iteration == 0, iteration == ITERS - 1
        pieces, inner = partial_image(covariance, lowered, order, index, cols, first)
        own, got, (here, before, inner) = exchange_sum(pieces, rows, (residual, earlier, inner))
        norm = local_norm(here)
        if first:
            own, norm = lax.optimization_barrier((own, norm))
            inner_residual = sum(inner[1:], inner[0]).astype(jnp.float32)
            blocks = [inner_residual]
            inner_direction = inner_residual
        else:
            iterate = advance(iterate, before, alpha)
            own, norm, iterate = lax.optimization_barrier((own, norm, iterate))
            blocks = [inner_residual, inner_direction]
        inner_image, grams = local_grams(own, got, norm, blocks)
        grams, image = sum_all(grams, rows, cols, inner_image, hops)
        alpha, beta = solve_small(grams, first)
        earlier = direction
        residual, direction, lowered = update(residual, direction, image, alpha, beta)
        if not last:
            inner_residual, inner_direction, _ = update(
                inner_residual, inner_direction, inner_image, alpha, beta
            )
    return (advance(iterate, earlier, alpha), residual, direction)


def solution(mesh):
    place = P(("col", "row"), None)
    return jax.shard_map(
        functools.partial(body, mesh.shape["row"], mesh.shape["col"]),
        mesh=mesh,
        in_specs=(P("row", "col"), place),
        out_specs=(place, place, place),
        check_vma=False,
    )
```
